256 devices in a mesh: ctx: 16 (over y_lo, x, core), tp: 16 (over y_hi, z).
Axes of the slice: x: 4, y: 4 (y_hi: 2, y_lo: 2; y = y_hi * 2 + y_lo), z: 8, core: 2. Of those that a mesh axis runs over, the one named last changes fastest.
Arguments:
- queries: bfloat16 [4096, 8192], P('ctx', 'tp'), may hold values from -6 to 6
- keys_copied: bfloat16 [4096, 2048], P('ctx', 'tp'), may hold values from -6 to 6, as said below
- values_copied: bfloat16 [4096, 2048], P('ctx', 'tp'), may hold values from -6 to 6, as said below
- attention_output_saved: bfloat16 [4096, 8192], P('ctx', 'tp'), may hold values from -6 to 6
- log_norm: float32 [64, 4096], P('tp', 'ctx'), as said below
- block_output_gradient: bfloat16 [4096, 8192], P(('ctx', 'tp')), may hold values from -6 to 6
- w_out: bfloat16 [8192, 8192], P('tp'), may hold values from -0.0625 to 0.0625
- adapter_down_factor: bfloat16 [8192, 64], P('tp'), may hold values from -0.0625 to 0.0625
- adapter_up: bfloat16 [64, 8192], replicated, may hold values from -0.0625 to 0.0625
Outputs:
- grad_query: bfloat16 [4096, 8192], P('ctx', 'tp')
- grad_keys: bfloat16 [4096, 2048], P('ctx', 'tp')
- grad_values: bfloat16 [4096, 2048], P('ctx', 'tp')
- down_factor_gradient: float32 [8192, 64], P('tp')
- up_factor_gradient: bfloat16 [64, 8192], replicated
The draws below stay inside these ranges and needn't reach their ends.
Inputs may be any that keep to these rules, and one draw needn't show every extreme that they name: log_norm[h, r] minus the natural logarithm of (1 + pos(r)) lies between 0 and 1.5. `keys_copied`: for every g below 8, the 128 columns from 2 * g * 128 equal the 128 columns that follow them. `values_copied`: for every g below 8, the 128 columns from 2 * g * 128 equal the 128 columns that follow them.
All inputs are finite; a program needn't handle non-finite values.
Results may differ from the reference program's by a relative error of at most 0.022.
Values may be sent and summed in bfloat16 or wider, within the bound.
No kernel may reach another device: no remote copies, remote signals or barrier semaphores. Data moves between devices by JAX's collectives and lax.ppermute only.
A program may use at most 64 MiB of HBM per device.

```python
import jax
import jax.numpy as jnp
from jax import lax

D = 8192
HD = 128
GROUP = 8
RANK = 64
TOK_DEV = 256
HEADS = 64
KVH = 8
TOKENS = 4096
N_CTX = 16


def copied_heads(key):
    normal_draw = jax.random.normal(key, (TOKENS, KVH, 1, HD), jnp.float32)
    normal_draw = jnp.clip(normal_draw, -6.0, 6.0)
    doubled = jnp.broadcast_to(normal_draw, (TOKENS, KVH, 2, HD))
    return doubled.reshape(TOKENS, 2 * KVH * HD)


def draw_keys_copied(key, part):
    key = jax.random.fold_in(key, 21)
    return copied_heads(key).astype(jnp.bfloat16)


def draw_values_copied(key, part):
    key = jax.random.fold_in(key, 37)
    return copied_heads(key).astype(jnp.bfloat16)


def draw_log_norm(key, part):
    key = jax.random.fold_in(key, 11)
    row_ids = jnp.arange(TOKENS, dtype=jnp.int32)
    device_count = TOKENS // TOK_DEV
    device = row_ids // TOK_DEV
    offset_rows = row_ids % TOK_DEV
    half_rows = TOK_DEV // 2
    early_pos = device * half_rows + offset_rows
    late_pos = (2 * device_count - 1 - device) * half_rows + offset_rows - half_rows
    positions = jnp.where(offset_rows < half_rows, early_pos, late_pos)
    baseline = jnp.log(positions.astype(jnp.float32) + 1.0)
    extra = jax.random.uniform(key, (HEADS, TOKENS), jnp.float32, 0.25, 1.0)
    return baseline[None, :] + extra


def steps_of(stream_key, extent, shards, smallest, largest):
    def one(axis_at, parts):
        draws = jax.random.uniform(jax.random.fold_in(jax.random.fold_in(stream_key, 6), axis_at), (parts,), jnp.float32, smallest / len(shards), largest / len(shards))
        return jnp.repeat(jnp.exp(draws), extent[axis_at] // parts).reshape((-1,) + (1,) * (len(extent) - axis_at - 1))

    loudness = one(*shards[0])
    for cut in shards[1:]:
        loudness = loudness * one(*cut)
    return loudness


def scatter_about(rng, shape, scale, limit, pieces=(), held_as=jnp.bfloat16):
    gain = steps_of(rng, shape, pieces, -0.22, 0.18) if pieces else 1.0
    drawn = jax.random.normal(rng, shape, jnp.float32) * scale * gain
    return jnp.minimum(jnp.maximum(drawn, -limit), limit).astype(held_as)


def setup_inputs(seed: int = 0) -> dict:
    keys = jax.random.split(jax.random.key(seed), 10)
    return {
        "queries": scatter_about(keys[0], (TOKENS, HEADS * HD), 1.0, 6.0, ((0, 16), (1, 16))),
        "keys_copied": draw_keys_copied(jax.random.fold_in(keys[9], 71), 0),
        "values_copied": draw_values_copied(jax.random.fold_in(keys[9], 71), 0),
        "attention_output_saved": scatter_about(keys[3], (TOKENS, HEADS * HD), 1.0, 6.0, ((0, 16), (1, 16))),
        "log_norm": draw_log_norm(jax.random.fold_in(keys[9], 71), 0),
        "block_output_gradient": scatter_about(keys[5], (TOKENS, D), 1.0, 6.0, ((0, 256),)),
        "w_out": scatter_about(keys[6], (HEADS * HD, D), (HEADS * HD) ** -0.5, 0.0625, ((0, 16),)),
        "adapter_down_factor": scatter_about(keys[7], (HEADS * HD, RANK), (HEADS * HD) ** -0.5, 0.0625, ((0, 16),)),
        "adapter_up": scatter_about(keys[8], (RANK, D), D ** -0.5, 0.0625),
    }


adapter_scale_factor = 2.0


def folded_positions():
    row_ids = jnp.arange(TOKENS, dtype=jnp.int32)
    device = row_ids // TOK_DEV
    offset_rows = row_ids % TOK_DEV
    half_rows = TOK_DEV // 2
    early_pos = device * half_rows + offset_rows
    late_pos = (2 * N_CTX - 1 - device) * half_rows + offset_rows - half_rows
    return jnp.where(offset_rows < half_rows, early_pos, late_pos)


def reference(queries, keys_copied, values_copied, attention_output_saved, log_norm, block_output_gradient, w_out, adapter_down_factor, adapter_up):
    adapter_cotangent_rows = jnp.dot(block_output_gradient, adapter_up.T, preferred_element_type=jnp.float32).astype(jnp.bfloat16)
    frozen_weight_gradient = jnp.dot(block_output_gradient, w_out.T, preferred_element_type=jnp.float32)
    adapter_input_gradient = jnp.dot(adapter_cotangent_rows, adapter_down_factor.T, preferred_element_type=jnp.float32)
    attention_output_gradient = (frozen_weight_gradient + adapter_scale_factor * adapter_input_gradient).astype(jnp.bfloat16)
    mixed_heads_rows = jnp.dot(attention_output_saved, adapter_down_factor, preferred_element_type=jnp.float32).astype(jnp.bfloat16)
    up_factor_gradient = (adapter_scale_factor * jnp.dot(mixed_heads_rows.T, block_output_gradient, preferred_element_type=jnp.float32)).astype(jnp.bfloat16)
    down_factor_gradient = adapter_scale_factor * jnp.dot(attention_output_saved.T, adapter_cotangent_rows, preferred_element_type=jnp.float32)
    product = attention_output_gradient.astype(jnp.float32) * attention_output_saved.astype(jnp.float32)
    row_delta = jnp.sum(product.reshape(TOKENS, HEADS, HD), axis=2)
    positions = folded_positions()
    visible = positions[:, None] >= positions[None, :]
    softmax_scale = HD ** -0.5
    half_group = GROUP // 2

    def one_group(group_index):
        def one_head(sums, member):
            head = group_index * GROUP + member
            column = (2 * group_index + member // half_group) * HD
            keys_head = lax.dynamic_slice_in_dim(keys_copied, column, HD, 1)
            values_head = lax.dynamic_slice_in_dim(values_copied, column, HD, 1)
            query_head = lax.dynamic_slice_in_dim(queries, head * HD, HD, 1)
            grad_head = lax.dynamic_slice_in_dim(attention_output_gradient, head * HD, HD, 1)
            norm_row = lax.dynamic_slice_in_dim(log_norm, head, 1, 0)[0]
            delta_row = lax.dynamic_slice_in_dim(row_delta, head, 1, 1)[:, 0]
            scores = jnp.dot(query_head, keys_head.T, preferred_element_type=jnp.float32) * softmax_scale
            attn_prob = jnp.where(visible, jnp.exp(scores - norm_row[:, None]), jnp.float32(0.0))
            probs_low = attn_prob.astype(jnp.bfloat16)
            value_grad = jnp.dot(probs_low.T, grad_head, preferred_element_type=jnp.float32)
            prob_grad = jnp.dot(grad_head, values_head.T, preferred_element_type=jnp.float32)
            score_grad = (attn_prob * (prob_grad - delta_row[:, None])).astype(jnp.bfloat16)
            query_grad = (jnp.dot(score_grad, keys_head, preferred_element_type=jnp.float32) * softmax_scale).astype(jnp.bfloat16)
            key_grad = jnp.dot(score_grad.T, query_head, preferred_element_type=jnp.float32) * softmax_scale
            return (sums[0] + key_grad, sums[1] + value_grad), query_grad

        zero_sums = (jnp.zeros((TOKENS, HD), jnp.float32), jnp.zeros((TOKENS, HD), jnp.float32))
        sums, query_grads = lax.scan(one_head, zero_sums, jnp.arange(GROUP, dtype=jnp.int32))
        return sums[0].astype(jnp.bfloat16), sums[1].astype(jnp.bfloat16), query_grads

    key_grads, value_grads, query_grads = lax.map(one_group, jnp.arange(KVH, dtype=jnp.int32))
    grad_query = jnp.transpose(query_grads, (2, 0, 1, 3)).reshape(TOKENS, HEADS * HD)
    key_twice = jnp.repeat(key_grads, 2, axis=0)
    value_twice = jnp.repeat(value_grads, 2, axis=0)
    grad_keys = jnp.transpose(key_twice, (1, 0, 2)).reshape(TOKENS, 2 * KVH * HD)
    grad_values = jnp.transpose(value_twice, (1, 0, 2)).reshape(TOKENS, 2 * KVH * HD)
    return grad_query, grad_keys, grad_values, down_factor_gradient, up_factor_gradient
```

```python
import functools

import jax
import jax.numpy as jnp
from jax import lax
from jax.experimental import pallas as pl
from jax.experimental.pallas import tpu as pltpu
from jax.sharding import Mesh, PartitionSpec as P

CTX = ("ylo", "x", "core")
TP = ("yhi", "z")
SIZES = (2, 4, 2, 2, 8)
ADAPTER_SCALE = 2.0
LOG2E = 1.4426950408889634
F32 = jnp.float32
BF16 = jnp.bfloat16
HALF = 128
HEAD_DIM = 128
LAST = (((1,), (1,)), ((), ()))
FIRST = (((0,), (0,)), ((), ()))


def turned(x, axis, by):
    size = lax.axis_size(axis)
    return lax.ppermute(x, axis, [(i, (i + by) % size) for i in range(size)])


def rolled(x, by, axis=0):
    size = x.shape[axis]
    twice = jnp.concatenate([x, x], axis)
    return lax.dynamic_slice_in_dim(twice, by, size, axis)


def gathered_round(x, axis):
    up, down, blocks = x, x, {0: x}
    for step in range(1, 4):
        up, down = turned(up, axis, 1), turned(down, axis, -1)
        blocks[8 - step], blocks[step] = up, down
    cut = x.shape[1] // 256 * 128
    blocks[4] = jnp.concatenate(
        [turned(up[:, :cut], axis, 1), turned(down[:, cut:], axis, -1)], 1
    )
    return [blocks[j] for j in range(8)]


def gathered_keys_values(kv):
    ylo, x, core = (lax.axis_index(a) for a in CTX)
    two = jnp.stack([kv, turned(kv, "ylo", 1)])
    left, right = turned(two, "x", 1), turned(two, "x", -1)
    far = jnp.concatenate([turned(left[0:1], "x", 1), turned(right[1:2], "x", -1)])
    four = rolled(jnp.stack([two, right, far, left]), 4 - x)
    other = turned(four, "core", 1)
    first = jnp.where(core == 0, four, other)
    second = jnp.where(core == 0, other, four)
    both = jnp.stack([first, second], 2)
    both = jnp.swapaxes(both, 0, 1)
    both = jnp.where(ylo == 0, both, both[::-1])
    return both.reshape(16, 256, 256)


def attention_kernel(
    where_ref, q_ref, o_ref, g_ref, norm_ref, kv_ref, dq_ref, dkv_ref, qs, gs, norm, delta, dq_sum
):
    c = where_ref[0]
    heads = q_ref.shape[1] // HEAD_DIM
    scale = HEAD_DIM**-0.5
    for half in range(2):
        rows = slice(half * HALF, (half + 1) * HALF)
        for h in range(heads):
            cols = slice(h * HEAD_DIM, (h + 1) * HEAD_DIM)
            into = slice(h * HALF, (h + 1) * HALF)
            g = g_ref[rows, cols]
            qs[half, into, :] = q_ref[rows, cols]
            gs[half, into, :] = g
            product = g.astype(F32) * o_ref[rows, cols].astype(F32)
            delta[half, :, into] = jnp.sum(product.T, axis=0, keepdims=True)
            norm[half, :, into] = norm_ref[h : h + 1, rows] * LOG2E
    dq_sum[...] = jnp.zeros_like(dq_sum)
    dkv_ref[:, HALF:, :] = jnp.zeros((16, HALF, 2 * HEAD_DIM), BF16)

    def tile(half, keys, values, visible):
        q, g = qs[half], gs[half]
        scores = lax.dot_general(keys, q, LAST, preferred_element_type=F32)
        prob = jnp.exp2(scores * (scale * LOG2E) - norm[half])
        if visible is not None:
            prob = jnp.where(visible, prob, 0.0)
        prob_grad = lax.dot_general(values, g, LAST, preferred_element_type=F32)
        score_grad = (prob * (prob_grad - delta[half])).astype(BF16)
        value_grad = jnp.dot(prob.astype(BF16), g, preferred_element_type=F32)
        key_grad = jnp.dot(score_grad, q, preferred_element_type=F32) * scale
        query_grad = lax.dot_general(score_grad, keys, FIRST, preferred_element_type=F32)
        return query_grad, key_grad, value_grad

    def late_rows(step, carry):
        s = step * 2
        keys = kv_ref[pl.ds(s, 2), :HALF, :HEAD_DIM].reshape(2 * HALF, HEAD_DIM)
        values = kv_ref[pl.ds(s, 2), :HALF, HEAD_DIM:].reshape(2 * HALF, HEAD_DIM)
        query_grad, key_grad, value_grad = tile(1, keys, values, None)
        dq_sum[1] += query_grad
        dkv_ref[pl.ds(s, 2), :HALF, :HEAD_DIM] = key_grad.astype(BF16).reshape(2, HALF, HEAD_DIM)
        dkv_ref[pl.ds(s, 2), :HALF, HEAD_DIM:] = value_grad.astype(BF16).reshape(2, HALF, HEAD_DIM)
        return carry

    lax.fori_loop(0, 8, late_rows, 0)

    key_at = lax.broadcasted_iota(jnp.int32, (HALF, heads * HALF), 0)
    query_at = lax.broadcasted_iota(jnp.int32, (HALF, heads * HALF), 1) % HALF
    ahead = query_at - key_at

    def own_part(i, carry):
        late = (i > c).astype(jnp.int32)
        s = i - late
        first = pl.multiple_of(late * HALF, HALF)
        visible = ahead >= jnp.where(s == c, 0, -HALF)
        keys = kv_ref[s, pl.ds(first, HALF), :HEAD_DIM]
        values = kv_ref[s, pl.ds(first, HALF), HEAD_DIM:]
        query_grad, key_grad, value_grad = tile(late, keys, values, visible)
        dq_sum[late] += query_grad
        before = dkv_ref[s, pl.ds(first, HALF), :].astype(F32)
        now = jnp.concatenate([key_grad, value_grad], 1)
        dkv_ref[s, pl.ds(first, HALF), :] = (before + now).astype(BF16)
        return carry

    lax.fori_loop(0, 17, own_part, 0)
    for half in range(2):
        for h in range(heads):
            dq_ref[half * HALF : (half + 1) * HALF, h * HEAD_DIM : (h + 1) * HEAD_DIM] = (
                dq_sum[half, h * HALF : (h + 1) * HALF, :] * scale
            ).astype(BF16)


def attention(c, q, o, g, norm, kv):
    rows, width = q.shape
    vmem = pl.BlockSpec(memory_space=pltpu.VMEM)
    side = width // HEAD_DIM * HALF
    return pl.pallas_call(
        attention_kernel,
        out_shape=(
            jax.ShapeDtypeStruct((rows, width), BF16),
            jax.ShapeDtypeStruct(kv.shape, BF16),
        ),
        in_specs=[pl.BlockSpec(memory_space=pltpu.SMEM)] + [vmem] * 5,
        out_specs=(vmem, vmem),
        scratch_shapes=[
            pltpu.VMEM((2, side, HEAD_DIM), BF16),
            pltpu.VMEM((2, side, HEAD_DIM), BF16),
            pltpu.VMEM((2, 1, side), F32),
            pltpu.VMEM((2, 1, side), F32),
            pltpu.VMEM((2, side, HEAD_DIM), F32),
        ],
        compiler_params=pltpu.CompilerParams(vmem_limit_bytes=24 * 1024 * 1024),
        cost_estimate=pl.CostEstimate(
            flops=3 * 10**9, bytes_accessed=5 * 2**20, transcendentals=3 * 10**6
        ),
    )(jnp.reshape(c, (1,)).astype(jnp.int32), q, o, g, norm, kv)


def local(q, k, v, o, log_norm, dy, w, down, up):
    ylo, x, core, yhi, z = (lax.axis_index(a) for a in CTX + TP)
    c = ylo * 8 + x * 2 + core
    kv = gathered_keys_values(jnp.concatenate([k, v], 1))
    mixed = jnp.dot(o, down, preferred_element_type=F32).astype(BF16).reshape(16, 1024)
    cot = lax.dot_general(dy, up, LAST, preferred_element_type=F32).astype(BF16)
    message = jnp.concatenate([dy, mixed, cot, jnp.zeros((16, 64), BF16)], 1)
    peer = turned(dy, "yhi", 1)
    own_blocks = gathered_round(message, "z")
    peer_blocks = gathered_round(peer, "z")
    own_rows = jnp.concatenate([b[:, :8192] for b in own_blocks])
    peer_rows = jnp.concatenate(peer_blocks)
    own_mixed = sum(b[:, 8192:9216].astype(F32) for b in own_blocks)
    own_cot = jnp.concatenate([b[:, 9216:9280] for b in own_blocks]).reshape(8, 1024)
    own_cot = rolled(own_cot, 8 - z)
    sent = lax.dynamic_slice_in_dim(own_mixed, (1 - yhi) * 8, 8, 0).astype(BF16)
    received = turned(jnp.concatenate([sent, own_cot]), "yhi", 1)
    half_mixed = lax.dynamic_slice_in_dim(own_mixed, yhi * 8, 8, 0) + received[:8].astype(F32)
    half_mixed = rolled(half_mixed.astype(BF16), z).reshape(128, 64)
    peer_cot = received[8:]
    all_cot = jnp.concatenate([own_cot, peer_cot])
    all_cot = jnp.where(yhi == 0, all_cot, jnp.roll(all_cot, 8, 0)).reshape(256, 64)
    columns = lax.dynamic_slice_in_dim(own_rows, z * 1024, 1024, 1)
    up_part = ADAPTER_SCALE * lax.dot_general(half_mixed, columns, FIRST, preferred_element_type=F32)
    down_part = ADAPTER_SCALE * lax.dot_general(all_cot, o, FIRST, preferred_element_type=F32)
    parts = jnp.stack(
        [
            jnp.concatenate([up_part[:, i * 512 : i * 512 + 512], down_part[:, i * 256 : i * 256 + 256]], 1)
            for i in range(2)
        ]
    )
    mine = lax.dynamic_index_in_dim(parts, core, 0, False)
    yours = lax.dynamic_index_in_dim(parts, 1 - core, 0, False).astype(BF16)
    total = mine + turned(yours, "core", 1).astype(F32)
    total = total + turned(total.astype(BF16), "ylo", 1).astype(F32)
    low = total.astype(BF16)
    total = total + lax.ppermute(low, "x", [(i, i ^ 1) for i in range(4)]).astype(F32)
    low = total.astype(BF16)
    total = total + lax.ppermute(low, "x", [(i, 3 - i) for i in range(4)]).astype(F32)
    down_total, up_total = total[:, 512:], total[:, :512]
    up_total = up_total + turned(up_total.astype(BF16), "yhi", 1).astype(F32)
    up_blocks = jnp.concatenate(gathered_round(up_total.astype(BF16), "z"), 1)
    mine = jnp.concatenate([up_blocks, down_total.astype(BF16)], 1)
    yours = turned(mine, "core", 1)
    pair = jnp.stack([jnp.where(core == 0, mine, yours), jnp.where(core == 0, yours, mine)])
    up_grad = jnp.swapaxes(pair[:, :, :4096].reshape(2, 64, 8, 512), 0, 1)
    up_grad = jnp.swapaxes(up_grad, 1, 2)
    up_grad = rolled(up_grad, 8 - z, 1).reshape(64, 8192)
    down_grad = jnp.swapaxes(pair[:, :, 4096:], 1, 2).reshape(512, 64).astype(F32)
    own_product = lax.dot_general(own_rows, w, LAST, preferred_element_type=F32)
    peer_product = lax.dot_general(peer_rows, w, LAST, preferred_element_type=F32)
    own_product = rolled(own_product, (8 - z) * 16)
    peer_product = rolled(peer_product, (8 - z) * 16)
    product = jnp.concatenate([own_product, peer_product, own_product])
    product = lax.dynamic_slice_in_dim(product, yhi * 128, 256, 0)
    through_adapter = lax.dot_general(all_cot, down, LAST, preferred_element_type=F32)
    g = (product + ADAPTER_SCALE * through_adapter).astype(BF16)
    dq, dkv = attention(c, q, o, g, log_norm, kv)
    pieces = lax.all_to_all(dkv, CTX, 0, 0)
    dkv_sum = jnp.sum(pieces.astype(F32), 0)
    other = lax.ppermute(dkv_sum.astype(BF16), "z", [(i, i ^ 1) for i in range(8)])
    dkv_sum = (dkv_sum + other.astype(F32)).astype(BF16)
    return dq, dkv_sum[:, :128], dkv_sum[:, 128:], down_grad, up_grad


def solution(mesh):
    fine = Mesh(mesh.devices.reshape(SIZES), CTX + TP)
    placed = (
        P(CTX, TP),
        P(CTX, TP),
        P(CTX, TP),
        P(CTX, TP),
        P(TP, CTX),
        P(CTX + TP, None),
        P(TP, None),
        P(TP, None),
        P(),
    )
    return jax.shard_map(
        local,
        mesh=fine,
        in_specs=placed,
        out_specs=(P(CTX, TP), P(CTX, TP), P(CTX, TP), P(TP, None), P()),
        check_vma=False,
    )
```

```python
import functools

import jax
import jax.numpy as jnp
from jax import lax
from jax.experimental import pallas as pl
from jax.experimental.pallas import tpu as pltpu
from jax.sharding import Mesh, PartitionSpec as P

CTX = ("ylo", "x", "core")
TP = ("yhi", "z")
SIZES = (2, 4, 2, 2, 8)
ADAPTER_SCALE = 2.0
LOG2E = 1.4426950408889634
F32 = jnp.float32
BF16 = jnp.bfloat16
HALF = 128
HEAD_DIM = 128
LAST = (((1,), (1,)), ((), ()))
FIRST = (((0,), (0,)), ((), ()))


def turned(x, axis, by):
    size = lax.axis_size(axis)
    return lax.ppermute(x, axis, [(i, (i + by) % size) for i in range(size)])


def rolled(x, by, axis=0):
    size = x.shape[axis]
    twice = jnp.concatenate([x, x], axis)
    return lax.dynamic_slice_in_dim(twice, by, size, axis)


def gathered_round(x, axis, far_up, before_last=lambda up, down: (up, down)):
    up, down, blocks = x, x, {0: x}
    for step in range(1, 4):
        up, down = turned(up, axis, 1), turned(down, axis, -1)
        blocks[8 - step], blocks[step] = up, down
    up, down = before_last(up, down)
    blocks[4] = turned(up, axis, 1) if far_up else turned(down, axis, -1)
    return [blocks[j] for j in range(8)]


def place_kernel(where_ref, *refs):
    blocks, out_ref = refs[:-1], refs[-1]
    width = blocks[0].shape[1]
    for j, block in enumerate(blocks):
        to = pl.multiple_of(lax.rem(where_ref[2] + j, len(blocks)) * width, 128)
        out_ref[:, pl.ds(to, width)] = block[...]


def placed_round(where, blocks):
    rows, width = blocks[0].shape
    vmem = pl.BlockSpec(memory_space=pltpu.VMEM)
    return pl.pallas_call(
        place_kernel,
        out_shape=jax.ShapeDtypeStruct((rows, width * len(blocks)), blocks[0].dtype),
        in_specs=[pl.BlockSpec(memory_space=pltpu.SMEM)] + [vmem] * len(blocks),
        out_specs=vmem,
        compiler_params=pltpu.CompilerParams(vmem_limit_bytes=16 * 1024 * 1024),
        cost_estimate=pl.CostEstimate(flops=0, bytes_accessed=2**20, transcendentals=0),
    )(where, *blocks)


def sum_kernel(pieces_ref, sum_ref, low_ref):
    total = pieces_ref[0].astype(F32)
    for i in range(1, pieces_ref.shape[0]):
        total += pieces_ref[i].astype(F32)
    sum_ref[...] = total
    low_ref[...] = total.astype(BF16)


def summed(pieces):
    vmem = pl.BlockSpec(memory_space=pltpu.VMEM)
    return pl.pallas_call(
        sum_kernel,
        out_shape=(
            jax.ShapeDtypeStruct(pieces.shape[1:], F32),
            jax.ShapeDtypeStruct(pieces.shape[1:], BF16),
        ),
        in_specs=[vmem],
        out_specs=(vmem, vmem),
        compiler_params=pltpu.CompilerParams(vmem_limit_bytes=16 * 1024 * 1024),
        cost_estimate=pl.CostEstimate(flops=2 * 10**10, bytes_accessed=2**21, transcendentals=0),
    )(pieces)


STEP = 1024
AHEAD = 3


def row_copies(blocks, rows, sems, z):
    copies = []
    for j, block in enumerate(blocks):
        to = pl.multiple_of(lax.rem(z + j, 8) * 16, 16)
        width = rows.shape[1]
        copies.append(
            pltpu.make_async_copy(block.at[:, :width], rows.at[pl.ds(to, 16), :], sems.at[j])
        )
    return copies


def column_copies(source, to, sems):
    return [
        pltpu.make_async_copy(
            source.at[:, i * STEP : (i + 1) * STEP], to.at[:, i * STEP : (i + 1) * STEP], sems.at[i]
        )
        for i in range(source.shape[1] // STEP)
    ]


def product_of(rows, row_copy, w, w_copy):
    for copy in row_copy + w_copy[:AHEAD]:
        copy.start()
    for copy in row_copy:
        copy.wait()
    product = None
    for i, copy in enumerate(w_copy):
        copy.wait()
        for later in w_copy[i + AHEAD : i + AHEAD + 1]:
            later.start()
        at = slice(i * STEP, (i + 1) * STEP)
        term = lax.dot_general(rows[:, at], w[:, at], LAST, preferred_element_type=F32)
        product = term if product is None else product + term
    return product


def cotangent_of(rows, up):
    cots = None
    for i in range(up.shape[1] // STEP):
        at = slice(i * STEP, (i + 1) * STEP)
        term = lax.dot_general(rows[:, at], up[:, at], LAST, preferred_element_type=F32)
        cots = term if cots is None else cots + term
    return cots.astype(BF16)


def own_kernel(where_ref, *refs):
    blocks, (w_ref, up_ref, product_ref, cots_ref, chunk_ref) = refs[:8], refs[8:13]
    rows, w, up, row_sems, w_sems, up_sems = refs[13:]
    z = where_ref[2]
    row_copy = row_copies(blocks, rows, row_sems, z)
    product_ref[...] = product_of(rows, row_copy, w, column_copies(w_ref, w, w_sems))
    up_copy = column_copies(up_ref, up, up_sems)
    for copy in up_copy:
        copy.start()
    for copy in up_copy:
        copy.wait()
    cots_ref[...] = cotangent_of(rows, up)
    chunk_ref[...] = rows[:, pl.ds(pl.multiple_of(z * 1024, 1024), 1024)]


def own_call(where, blocks, w, up):
    vmem = pl.BlockSpec(memory_space=pltpu.VMEM)
    anywhere = pl.BlockSpec(memory_space=pl.ANY)
    hbm = pl.BlockSpec(memory_space=pltpu.HBM)
    rank, width = up.shape
    return pl.pallas_call(
        own_kernel,
        out_shape=(
            jax.ShapeDtypeStruct((128, w.shape[0]), F32),
            jax.ShapeDtypeStruct((128, rank), BF16),
            jax.ShapeDtypeStruct((128, 1024), BF16),
        ),
        in_specs=[pl.BlockSpec(memory_space=pltpu.SMEM)] + [anywhere] * 8 + [hbm] * 2,
        out_specs=(vmem,) * 3,
        scratch_shapes=[
            pltpu.VMEM((128, width), BF16),
            pltpu.VMEM(w.shape, BF16),
            pltpu.VMEM((rank, width), BF16),
            pltpu.SemaphoreType.DMA((8,)),
            pltpu.SemaphoreType.DMA((width // STEP,)),
            pltpu.SemaphoreType.DMA((width // STEP,)),
        ],
        compiler_params=pltpu.CompilerParams(vmem_limit_bytes=54 * 1024 * 1024),
        cost_estimate=pl.CostEstimate(flops=8 * 10**9, bytes_accessed=2**23, transcendentals=0),
    )(where, *blocks, w, up)


def adapter_kernel(where_ref, *refs):
    peer = refs[:8]
    up_ref, chunk_ref, own_cots_ref, o_ref, cots_ref, mine_ref, yours_ref = refs[8:15]
    rows, up, tails, chunks, row_sems, tail_sems, up_sems = refs[15:]
    yhi, z, core = where_ref[1], where_ref[2], where_ref[3]
    copies = column_copies(up_ref, up, up_sems) + row_copies(peer, rows, row_sems, z)
    copies += [
        pltpu.make_async_copy(block.at[:, rows.shape[1] :], tails.at[j], tail_sems.at[j])
        for j, block in enumerate(peer)
    ]
    for copy in copies:
        copy.start()
    chunks[yhi] = chunk_ref[...]
    for copy in copies:
        copy.wait()
    mixed = tails[0].astype(F32)
    for j in range(1, 8):
        mixed += tails[j].astype(F32)
    mixed = mixed.astype(BF16)
    mixed = jnp.concatenate([mixed[:, i * 256 : i * 256 + 256] for i in range(4)])
    chunks[1 - yhi] = rows[:, pl.ds(pl.multiple_of(z * 1024, 1024), 1024)]
    peer_cots, own_cots = cotangent_of(rows, up), own_cots_ref[...]
    cots = jnp.concatenate(
        [jnp.where(yhi == 0, own_cots, peer_cots), jnp.where(yhi == 0, peer_cots, own_cots)]
    )
    cots_ref[...] = cots
    columns = chunks[...].reshape(256, 1024)
    up_part = ADAPTER_SCALE * jnp.dot(mixed, columns, preferred_element_type=F32)
    down_part = lax.dot_general(cots, o_ref[...], FIRST, preferred_element_type=F32)
    down_part = ADAPTER_SCALE * down_part
    first = jnp.concatenate([up_part[:, :512], down_part[:, :256]], 1)
    second = jnp.concatenate([up_part[:, 512:], down_part[:, 256:]], 1)
    mine_ref[...] = jnp.where(core == 0, first, second)
    yours_ref[...] = jnp.where(core == 0, second, first).astype(BF16)


def adapter_call(where, peer, up, chunk, own_cots, o):
    vmem = pl.BlockSpec(memory_space=pltpu.VMEM)
    anywhere = pl.BlockSpec(memory_space=pl.ANY)
    rank, width = up.shape
    return pl.pallas_call(
        adapter_kernel,
        out_shape=(
            jax.ShapeDtypeStruct((256, rank), BF16),
            jax.ShapeDtypeStruct((rank, 768), F32),
            jax.ShapeDtypeStruct((rank, 768), BF16),
        ),
        in_specs=[pl.BlockSpec(memory_space=pltpu.SMEM)]
        + [anywhere] * 8
        + [pl.BlockSpec(memory_space=pltpu.HBM)]
        + [vmem] * 3,
        out_specs=(vmem,) * 3,
        scratch_shapes=[
            pltpu.VMEM((128, width), BF16),
            pltpu.VMEM((rank, width), BF16),
            pltpu.VMEM((8, 16, 1024), BF16),
            pltpu.VMEM((2, 128, 1024), BF16),
            pltpu.SemaphoreType.DMA((8,)),
            pltpu.SemaphoreType.DMA((8,)),
            pltpu.SemaphoreType.DMA((width // STEP,)),
        ],
        compiler_params=pltpu.CompilerParams(vmem_limit_bytes=20 * 1024 * 1024),
        cost_estimate=pl.CostEstimate(flops=10**9, bytes_accessed=2**22, transcendentals=0),
    )(where, *peer, up, chunk, own_cots, o)


def peer_kernel(where_ref, *refs):
    blocks, (w_ref, own_ref, cots_ref, down_ref, g_ref) = refs[:8], refs[8:13]
    rows, w, own, cots, row_sems, w_sems, sems = refs[13:]
    small = [
        pltpu.make_async_copy(own_ref, own, sems.at[0]),
        pltpu.make_async_copy(cots_ref, cots, sems.at[1]),
    ]
    for copy in small:
        copy.start()
    yhi = where_ref[1]
    row_copy = row_copies(blocks, rows, row_sems, where_ref[2])
    product = product_of(rows, row_copy, w, column_copies(w_ref, w, w_sems))
    for copy in small:
        copy.wait()
    adapter = ADAPTER_SCALE * jnp.dot(cots[...], down_ref[...], preferred_element_type=F32)
    for half in range(2):
        part = jnp.where(yhi == half, own[...], product)
        g_ref[half] = (part + adapter[half * 128 : half * 128 + 128]).astype(BF16)


def peer_call(where, blocks, w, own, cots, down):
    vmem = pl.BlockSpec(memory_space=pltpu.VMEM)
    anywhere = pl.BlockSpec(memory_space=pl.ANY)
    width = w.shape[1]
    return pl.pallas_call(
        peer_kernel,
        out_shape=jax.ShapeDtypeStruct((2, 128, w.shape[0]), BF16),
        in_specs=[pl.BlockSpec(memory_space=pltpu.SMEM)]
        + [anywhere] * 8
        + [pl.BlockSpec(memory_space=pltpu.HBM), anywhere, anywhere, vmem],
        out_specs=vmem,
        scratch_shapes=[
            pltpu.VMEM((128, width), BF16),
            pltpu.VMEM(w.shape, BF16),
            pltpu.VMEM(own.shape, F32),
            pltpu.VMEM(cots.shape, BF16),
            pltpu.SemaphoreType.DMA((8,)),
            pltpu.SemaphoreType.DMA((width // STEP,)),
            pltpu.SemaphoreType.DMA((2,)),
        ],
        compiler_params=pltpu.CompilerParams(vmem_limit_bytes=54 * 1024 * 1024),
        cost_estimate=pl.CostEstimate(flops=8 * 10**9, bytes_accessed=2**23, transcendentals=0),
    )(where, *blocks, w, own, cots, down)


def tile(q, g, norm, delta, keys, values, visible):
    scale = HEAD_DIM**-0.5
    scores = lax.dot_general(keys, q, LAST, preferred_element_type=F32)
    prob = jnp.exp2(scores * (scale * LOG2E) - norm)
    if visible is not None:
        prob = jnp.where(visible, prob, 0.0)
    prob_grad = lax.dot_general(values, g, LAST, preferred_element_type=F32)
    score_grad = (prob * (prob_grad - delta)).astype(BF16)
    value_grad = jnp.dot(prob.astype(BF16), g, preferred_element_type=F32)
    key_grad = jnp.dot(score_grad, q, preferred_element_type=F32) * scale
    query_grad = lax.dot_general(score_grad, keys, FIRST, preferred_element_type=F32)
    return query_grad, key_grad, value_grad


def late_kernel(
    q_ref, o_ref, g_ref, norm_ref, kv_ref, qs, gs, norm, delta, dq_sum, dkv_ref
):
    heads = q_ref.shape[1] // HEAD_DIM
    for half in range(2):
        rows = slice(half * HALF, (half + 1) * HALF)
        for h in range(heads):
            cols = slice(h * HEAD_DIM, (h + 1) * HEAD_DIM)
            into = slice(h * HALF, (h + 1) * HALF)
            qs[half, into, :] = q_ref[rows, cols]
            norm[half, :, into] = norm_ref[h : h + 1, rows] * LOG2E
            g = g_ref[half, :, cols]
            gs[half, into, :] = g
            product = g.astype(F32) * o_ref[rows, cols].astype(F32)
            delta[half, :, into] = jnp.sum(product.T, axis=0, keepdims=True)
    dq_sum[0] = jnp.zeros_like(dq_sum[0])
    dkv_ref[:, HALF:, :] = jnp.zeros((16, HALF, 2 * HEAD_DIM), BF16)
    for s in range(0, 16, 2):
        keys = kv_ref[s : s + 2, :HALF, :HEAD_DIM].reshape(2 * HALF, HEAD_DIM)
        values = kv_ref[s : s + 2, :HALF, HEAD_DIM:].reshape(2 * HALF, HEAD_DIM)
        query_grad, key_grad, value_grad = tile(
            qs[1], gs[1], norm[1], delta[1], keys, values, None
        )
        if s:
            dq_sum[1] += query_grad
        else:
            dq_sum[1] = query_grad
        dkv_ref[s : s + 2, :HALF, :HEAD_DIM] = key_grad.astype(BF16).reshape(2, HALF, HEAD_DIM)
        dkv_ref[s : s + 2, :HALF, HEAD_DIM:] = value_grad.astype(BF16).reshape(2, HALF, HEAD_DIM)


def rest_kernel(
    where_ref, qs, gs, norm, delta, dq_in, kv_ref, dkv_in, dq_ref, mine_ref, yours_ref, dq_sum, dkv_ref
):
    c = where_ref[0]
    heads = dq_ref.shape[1] // HEAD_DIM
    scale = HEAD_DIM**-0.5
    dkv_ref[...] = dkv_in[...]
    dq_sum[...] = dq_in[...]
    key_at = lax.broadcasted_iota(jnp.int32, (HALF, heads * HALF), 0)
    query_at = lax.broadcasted_iota(jnp.int32, (HALF, heads * HALF), 1) % HALF
    ahead = query_at - key_at

    def unit(i):
        late = (i > c).astype(jnp.int32)
        s = i - late
        first = pl.multiple_of(late * HALF, HALF)
        visible = ahead >= jnp.where(s == c, 0, -HALF)
        keys = kv_ref[s, pl.ds(first, HALF), :HEAD_DIM]
        values = kv_ref[s, pl.ds(first, HALF), HEAD_DIM:]
        query_grad, key_grad, value_grad = tile(
            qs[late], gs[late], norm[late], delta[late], keys, values, visible
        )
        return late, s, first, query_grad, jnp.concatenate([key_grad, value_grad], 1)

    def stored(late, s, first, query_grad, now):
        dq_sum[late] += query_grad
        before = dkv_ref[s, pl.ds(first, HALF), :].astype(F32)
        dkv_ref[s, pl.ds(first, HALF), :] = (before + now).astype(BF16)

    for first in range(0, 17, 4):
        for done in [unit(i) for i in range(first, min(first + 4, 17))]:
            stored(*done)
    core = where_ref[3]
    for k in range(8):
        mine_ref[k] = dkv_ref[2 * k + core]
        yours_ref[k] = dkv_ref[2 * k + 1 - core]
    for half in range(2):
        for h in range(heads):
            dq_ref[half * HALF : (half + 1) * HALF, h * HEAD_DIM : (h + 1) * HEAD_DIM] = (
                dq_sum[half, h * HALF : (h + 1) * HALF, :] * scale
            ).astype(BF16)


def late_call(q, o, g, log_norm, kv):
    side = q.shape[1] // HEAD_DIM * HALF
    vmem = pl.BlockSpec(memory_space=pltpu.VMEM)
    stacked = jax.ShapeDtypeStruct((2, side, HEAD_DIM), BF16)
    line = jax.ShapeDtypeStruct((2, 1, side), F32)
    return pl.pallas_call(
        late_kernel,
        out_shape=(
            stacked,
            stacked,
            line,
            line,
            jax.ShapeDtypeStruct((2, side, HEAD_DIM), F32),
            jax.ShapeDtypeStruct(kv.shape, BF16),
        ),
        in_specs=[vmem] * 5,
        out_specs=(vmem,) * 6,
        compiler_params=pltpu.CompilerParams(vmem_limit_bytes=24 * 1024 * 1024),
        cost_estimate=pl.CostEstimate(
            flops=10**10, bytes_accessed=2**22, transcendentals=10**6
        ),
    )(q, o, g, log_norm, kv)


def rest_call(where, kept, kv):
    qs, gs, norm, delta, dq, dkv = kept
    side = qs.shape[1]
    vmem = pl.BlockSpec(memory_space=pltpu.VMEM)
    half = jax.ShapeDtypeStruct((dkv.shape[0] // 2, *dkv.shape[1:]), BF16)
    return pl.pallas_call(
        rest_kernel,
        out_shape=(jax.ShapeDtypeStruct((2 * HALF, side), BF16), half, half),
        in_specs=[pl.BlockSpec(memory_space=pltpu.SMEM)] + [vmem] * 7,
        out_specs=(vmem,) * 3,
        scratch_shapes=[
            pltpu.VMEM((2, side, HEAD_DIM), F32),
            pltpu.VMEM(dkv.shape, BF16),
        ],
        compiler_params=pltpu.CompilerParams(vmem_limit_bytes=24 * 1024 * 1024),
        cost_estimate=pl.CostEstimate(
            flops=10**10, bytes_accessed=2**22, transcendentals=10**6
        ),
    )(where, qs, gs, norm, delta, dq, kv, dkv)


def local(q, k, v, o, log_norm, dy, w, down, up):
    ylo, x, core, yhi, z = (lax.axis_index(a) for a in CTX + TP)
    where = jnp.stack([ylo * 8 + x * 2 + core, yhi, z, core]).astype(jnp.int32)
    together = lax.optimization_barrier
    own_blocks = gathered_round(dy, "z", True)
    mixed = lax.dot_general(down, o, (((0,), (1,)), ((), ())), preferred_element_type=F32)
    mixed = jnp.concatenate([mixed[i * 16 : i * 16 + 16] for i in range(4)], 1)
    peer = turned(dy, "yhi", 1)
    other = turned(mixed.astype(BF16), "yhi", 1)
    peer = jnp.concatenate([peer, (mixed + other.astype(F32)).astype(BF16)], 1)
    own, own_cots, chunk = own_call(where, own_blocks, w, up)
    peer_blocks = gathered_round(peer, "z", False)
    kv, _ = together((jnp.concatenate([k, v], 1), peer))
    kv = lax.all_to_all(jnp.broadcast_to(kv[None], (16,) + kv.shape), CTX, 0, 0)
    cots, mine, yours = adapter_call(where, peer_blocks, up, chunk, own_cots, o)
    low = (mine + turned(yours, "core", 1).astype(F32)).astype(BF16)
    blocks, cots, low = together((peer_blocks, cots, low))
    g = peer_call(where, blocks, w, own, cots, down.T)
    total = low.astype(F32) + turned(low, "ylo", 1).astype(F32)
    low, g = together((total.astype(BF16), g))
    kept = late_call(q, o, g, log_norm, kv)
    total = low.astype(F32) + lax.ppermute(low, "x", [(i, i ^ 1) for i in range(4)]).astype(F32)
    low, kept = together((total.astype(BF16), kept))
    dq, mine, yours = rest_call(where, kept, kv)
    total = low.astype(F32) + lax.ppermute(low, "x", [(i, 3 - i) for i in range(4)]).astype(F32)
    low, mine, yours = together((total.astype(BF16), mine, yours))
    mine = (mine.astype(F32) + turned(yours, "core", 1).astype(F32)).astype(BF16)
    pieces = lax.all_to_all(mine, CTX[:2], 0, 0)
    other = turned(low, "core", 1)
    first, second = jnp.where(core == 0, low, other), jnp.where(core == 0, other, low)
    down_grad = jnp.concatenate([first[:, 512:], second[:, 512:]], 1).astype(F32).T
    up_total = jnp.concatenate([first[:, :512], second[:, :512]], 1)
    up_grad = placed_round(where, gathered_round(up_total, "z", True))
    dkv_sum, low = summed(pieces)
    other = lax.ppermute(low, "z", [(i, i ^ 1) for i in range(8)])
    dkv_sum = (dkv_sum + other.astype(F32)).astype(BF16)
    return dq, dkv_sum[:, :128], dkv_sum[:, 128:], down_grad, up_grad


def solution(mesh):
    fine = Mesh(mesh.devices.reshape(SIZES), CTX + TP)
    placed = (
        P(CTX, TP),
        P(CTX, TP),
        P(CTX, TP),
        P(CTX, TP),
        P(TP, CTX),
        P(CTX + TP, None),
        P(TP, None),
        P(TP, None),
        P(),
    )
    return jax.shard_map(
        local,
        mesh=fine,
        in_specs=placed,
        out_specs=(P(CTX, TP), P(CTX, TP), P(CTX, TP), P(TP, None), P()),
        check_vma=False,
    )
```

```python
import functools

import jax
import jax.numpy as jnp
from jax import lax
from jax.experimental import pallas as pl
from jax.experimental.pallas import tpu as pltpu
from jax.sharding import Mesh, PartitionSpec as P

CTX = ("ylo", "x", "core")
TP = ("yhi", "z")
SIZES = (2, 4, 2, 2, 8)
ADAPTER_SCALE = 2.0
LOG2E = 1.4426950408889634
F32 = jnp.float32
BF16 = jnp.bfloat16
HALF = 128
HEAD_DIM = 128
LAST = (((1,), (1,)), ((), ()))
FIRST = (((0,), (0,)), ((), ()))


def turned(x, axis, by):
    size = lax.axis_size(axis)
    return lax.ppermute(x, axis, [(i, (i + by) % size) for i in range(size)])


def rolled(x, by, axis=0):
    size = x.shape[axis]
    twice = jnp.concatenate([x, x], axis)
    return lax.dynamic_slice_in_dim(twice, by, size, axis)


def gathered_round(x, axis, far_up, before_last=lambda up, down: (up, down)):
    up, down, blocks = x, x, {0: x}
    for step in range(1, 4):
        up, down = turned(up, axis, 1), turned(down, axis, -1)
        blocks[8 - step], blocks[step] = up, down
    up, down = before_last(up, down)
    blocks[4] = turned(up, axis, 1) if far_up else turned(down, axis, -1)
    return [blocks[j] for j in range(8)]


def place_kernel(where_ref, *refs):
    blocks, out_ref = refs[:-1], refs[-1]
    width = blocks[0].shape[1]
    at = 0
    for block in blocks:
        part = lax.rem(where_ref[2] + at // width, PARTS)
        to = pl.multiple_of(part * width + at % width, 128)
        out_ref[:, pl.ds(to, block.shape[1])] = block[...]
        at += block.shape[1]


def placed_round(where, blocks):
    rows, width = blocks[0].shape
    vmem = pl.BlockSpec(memory_space=pltpu.VMEM)
    return pl.pallas_call(
        place_kernel,
        out_shape=jax.ShapeDtypeStruct((rows, width * PARTS), blocks[0].dtype),
        in_specs=[pl.BlockSpec(memory_space=pltpu.SMEM)] + [vmem] * len(blocks),
        out_specs=vmem,
        compiler_params=pltpu.CompilerParams(vmem_limit_bytes=16 * 1024 * 1024),
        cost_estimate=pl.CostEstimate(flops=0, bytes_accessed=2**20, transcendentals=0),
    )(where, *blocks)


def sum_kernel(pieces_ref, sum_ref, low_ref):
    total = pieces_ref[0].astype(F32)
    for i in range(1, pieces_ref.shape[0]):
        total += pieces_ref[i].astype(F32)
    sum_ref[...] = total
    low_ref[...] = total.astype(BF16)


def summed(pieces):
    vmem = pl.BlockSpec(memory_space=pltpu.VMEM)
    return pl.pallas_call(
        sum_kernel,
        out_shape=(
            jax.ShapeDtypeStruct(pieces.shape[1:], F32),
            jax.ShapeDtypeStruct(pieces.shape[1:], BF16),
        ),
        in_specs=[vmem],
        out_specs=(vmem, vmem),
        compiler_params=pltpu.CompilerParams(vmem_limit_bytes=16 * 1024 * 1024),
        cost_estimate=pl.CostEstimate(flops=2 * 10**10, bytes_accessed=2**21, transcendentals=0),
    )(pieces)


STEP = 1024
PARTS = 4


def row_copies(blocks, rows, sems, z):
    width = rows.shape[1]
    copies = []
    for j, block in enumerate(blocks):
        to = pl.multiple_of(lax.rem(z + j, 8) * 16, 16)
        copies.append(
            pltpu.make_async_copy(block.at[:, :width], rows.at[pl.ds(to, 16), :], sems.at[j])
        )
    return copies


def column_copies(source, to, sems):
    return [
        pltpu.make_async_copy(
            source.at[:, i * STEP : (i + 1) * STEP], to.at[:, i * STEP : (i + 1) * STEP], sems.at[i]
        )
        for i in range(source.shape[1] // STEP)
    ]


def cotangent_of(rows, up):
    cots = None
    for i in range(up.shape[1] // STEP):
        at = slice(i * STEP, (i + 1) * STEP)
        term = lax.dot_general(rows[:, at], up[:, at], LAST, preferred_element_type=F32)
        cots = term if cots is None else cots + term
    return cots.astype(BF16)


def own_kernel(where_ref, *refs):
    blocks, (up_ref, rows, cots_ref) = refs[:8], refs[8:11]
    up, row_sems, up_sems = refs[11:]
    copies = row_copies(blocks, rows, row_sems, where_ref[2]) + column_copies(up_ref, up, up_sems)
    for copy in copies:
        copy.start()
    for copy in copies:
        copy.wait()
    cots_ref[...] = cotangent_of(rows, up)


def own_call(where, blocks, up):
    vmem = pl.BlockSpec(memory_space=pltpu.VMEM)
    anywhere = pl.BlockSpec(memory_space=pl.ANY)
    rank, width = up.shape
    return pl.pallas_call(
        own_kernel,
        out_shape=(
            jax.ShapeDtypeStruct((128, width), BF16),
            jax.ShapeDtypeStruct((128, rank), BF16),
        ),
        in_specs=[pl.BlockSpec(memory_space=pltpu.SMEM)] + [anywhere] * 9,
        out_specs=(vmem,) * 2,
        scratch_shapes=[
            pltpu.VMEM((rank, width), BF16),
            pltpu.SemaphoreType.DMA((8,)),
            pltpu.SemaphoreType.DMA((width // STEP,)),
        ],
        compiler_params=pltpu.CompilerParams(vmem_limit_bytes=48 * 1024 * 1024),
        cost_estimate=pl.CostEstimate(flops=2 * 10**9, bytes_accessed=2**22, transcendentals=0),
    )(where, *blocks, up)


def adapter_kernel(where_ref, *refs):
    peer = refs[:8]
    up_ref, own_ref, own_cots_ref, o_ref, rows, cots_ref, mine_ref, yours_ref = refs[8:16]
    up, tails, chunks, row_sems, tail_sems, up_sems = refs[16:]
    yhi, z, core = where_ref[1], where_ref[2], where_ref[3]
    copies = column_copies(up_ref, up, up_sems) + row_copies(peer, rows, row_sems, z)
    copies += [
        pltpu.make_async_copy(block.at[:, rows.shape[1] :], tails.at[j], tail_sems.at[j])
        for j, block in enumerate(peer)
    ]
    for copy in copies:
        copy.start()
    wide = chunks.shape[2]
    at = pl.ds(pl.multiple_of(lax.rem(z, PARTS) * wide, wide), wide)
    chunks[yhi] = own_ref[:, at]
    for copy in copies:
        copy.wait()
    mixed = tails[0].astype(F32)
    for j in range(1, 8):
        mixed += tails[j].astype(F32)
    mixed = mixed.astype(BF16)
    mixed = jnp.concatenate([mixed[:, i * 256 : i * 256 + 256] for i in range(4)])
    chunks[1 - yhi] = rows[:, at]
    peer_cots, own_cots = cotangent_of(rows, up), own_cots_ref[...]
    cots = jnp.concatenate(
        [jnp.where(yhi == 0, own_cots, peer_cots), jnp.where(yhi == 0, peer_cots, own_cots)]
    )
    cots_ref[...] = cots
    columns = chunks[...].reshape(256, wide)
    up_part = ADAPTER_SCALE * jnp.dot(mixed, columns, preferred_element_type=F32)
    down_part = lax.dot_general(cots, o_ref[...], FIRST, preferred_element_type=F32)
    down_part = ADAPTER_SCALE * down_part
    cut = wide // 2
    first = jnp.concatenate([up_part[:, :cut], down_part[:, :256]], 1)
    second = jnp.concatenate([up_part[:, cut:], down_part[:, 256:]], 1)
    mine_ref[...] = jnp.where(core == 0, first, second)
    yours_ref[...] = jnp.where(core == 0, second, first).astype(BF16)


def adapter_call(where, peer, up, own_rows, own_cots, o):
    vmem = pl.BlockSpec(memory_space=pltpu.VMEM)
    anywhere = pl.BlockSpec(memory_space=pl.ANY)
    rank, width = up.shape
    return pl.pallas_call(
        adapter_kernel,
        out_shape=(
            jax.ShapeDtypeStruct((128, width), BF16),
            jax.ShapeDtypeStruct((256, rank), BF16),
            jax.ShapeDtypeStruct((rank, width // PARTS // 2 + 256), F32),
            jax.ShapeDtypeStruct((rank, width // PARTS // 2 + 256), BF16),
        ),
        in_specs=[pl.BlockSpec(memory_space=pltpu.SMEM)] + [anywhere] * 9 + [vmem] * 3,
        out_specs=(vmem,) * 4,
        scratch_shapes=[
            pltpu.VMEM((rank, width), BF16),
            pltpu.VMEM((8, 16, 1024), BF16),
            pltpu.VMEM((2, 128, width // PARTS), BF16),
            pltpu.SemaphoreType.DMA((8,)),
            pltpu.SemaphoreType.DMA((8,)),
            pltpu.SemaphoreType.DMA((width // STEP,)),
        ],
        compiler_params=pltpu.CompilerParams(vmem_limit_bytes=24 * 1024 * 1024),
        cost_estimate=pl.CostEstimate(flops=2 * 10**9, bytes_accessed=2**22, transcendentals=0),
    )(where, *peer, up, own_rows, own_cots, o)


def gradient_kernel(where_ref, own_ref, peer_ref, w_ref, cots_ref, down_ref, g_ref):
    yhi = where_ref[1]
    product = None
    for i in range(w_ref.shape[1] // STEP):
        at = slice(i * STEP, (i + 1) * STEP)
        rows = jnp.concatenate([own_ref[:, at], peer_ref[:, at]])
        term = lax.dot_general(rows, w_ref[:, at], LAST, preferred_element_type=F32)
        product = term if product is None else product + term
    adapter = jnp.dot(cots_ref[...], down_ref[...], preferred_element_type=F32)
    adapter = ADAPTER_SCALE * adapter
    for half in range(2):
        part = jnp.where(yhi == half, product[:128], product[128:])
        g_ref[half] = (part + adapter[half * 128 : half * 128 + 128]).astype(BF16)


def gradient_call(where, own_rows, peer_rows, w, cots, down):
    vmem = pl.BlockSpec(memory_space=pltpu.VMEM)
    return pl.pallas_call(
        gradient_kernel,
        out_shape=jax.ShapeDtypeStruct((2, 128, w.shape[0]), BF16),
        in_specs=[pl.BlockSpec(memory_space=pltpu.SMEM)] + [vmem] * 5,
        out_specs=vmem,
        compiler_params=pltpu.CompilerParams(vmem_limit_bytes=20 * 1024 * 1024),
        cost_estimate=pl.CostEstimate(flops=10**10, bytes_accessed=2**23, transcendentals=0),
    )(where, own_rows, peer_rows, w, cots, down)


def tile(q, g, norm, delta, keys, values, visible):
    scale = HEAD_DIM**-0.5
    scores = lax.dot_general(keys, q, LAST, preferred_element_type=F32)
    prob = jnp.exp2(scores * (scale * LOG2E) - norm)
    if visible is not None:
        prob = jnp.where(visible, prob, 0.0)
    prob_grad = lax.dot_general(values, g, LAST, preferred_element_type=F32)
    score_grad = (prob * (prob_grad - delta)).astype(BF16)
    value_grad = jnp.dot(prob.astype(BF16), g, preferred_element_type=F32)
    key_grad = jnp.dot(score_grad, q, preferred_element_type=F32) * scale
    query_grad = lax.dot_general(score_grad, keys, FIRST, preferred_element_type=F32)
    return query_grad, key_grad, value_grad


def late_kernel(
    q_ref, o_ref, g_ref, norm_ref, kv_ref, other_kv_ref,
    qs, gs, norm, delta, dq_sum, dkv_ref, other_dkv_ref,
):
    heads = q_ref.shape[1] // HEAD_DIM
    for half in range(2):
        rows = slice(half * HALF, (half + 1) * HALF)
        for h in range(heads):
            cols = slice(h * HEAD_DIM, (h + 1) * HEAD_DIM)
            into = slice(h * HALF, (h + 1) * HALF)
            qs[half, into, :] = q_ref[rows, cols]
            norm[half, :, into] = norm_ref[h : h + 1, rows] * LOG2E
            g = g_ref[half, :, cols]
            gs[half, into, :] = g
            product = g.astype(F32) * o_ref[rows, cols].astype(F32)
            delta[half, :, into] = jnp.sum(product.T, axis=0, keepdims=True)
    dq_sum[0] = jnp.zeros_like(dq_sum[0])
    for source, to in ((kv_ref, dkv_ref), (other_kv_ref, other_dkv_ref)):
        to[:, HALF:, :] = jnp.zeros((8, HALF, 2 * HEAD_DIM), BF16)
        for k in range(0, 8, 2):
            keys = source[k : k + 2, :HALF, :HEAD_DIM].reshape(2 * HALF, HEAD_DIM)
            values = source[k : k + 2, :HALF, HEAD_DIM:].reshape(2 * HALF, HEAD_DIM)
            query_grad, key_grad, value_grad = tile(
                qs[1], gs[1], norm[1], delta[1], keys, values, None
            )
            if k or source is not kv_ref:
                dq_sum[1] += query_grad
            else:
                dq_sum[1] = query_grad
            key_grad = key_grad.astype(BF16).reshape(2, HALF, HEAD_DIM)
            value_grad = value_grad.astype(BF16).reshape(2, HALF, HEAD_DIM)
            to[k : k + 2, :HALF, :HEAD_DIM] = key_grad
            to[k : k + 2, :HALF, HEAD_DIM:] = value_grad


def rest_kernel(
    where_ref, qs, gs, norm, delta, dq_in, kv_ref, other_kv_ref, dkv_in, other_dkv_in,
    dq_ref, mine_ref, yours_ref, dq_sum, kv, dkv_ref,
):
    c, core = where_ref[0], where_ref[3]
    heads = dq_ref.shape[1] // HEAD_DIM
    scale = HEAD_DIM**-0.5
    kv[0], kv[1] = kv_ref[...], other_kv_ref[...]
    dkv_ref[0], dkv_ref[1] = dkv_in[...], other_dkv_in[...]
    dq_sum[...] = dq_in[...]
    key_at = lax.broadcasted_iota(jnp.int32, (HALF, heads * HALF), 0)
    query_at = lax.broadcasted_iota(jnp.int32, (HALF, heads * HALF), 1) % HALF
    ahead = query_at - key_at

    def unit(i):
        late = (i > c).astype(jnp.int32)
        s = i - late
        first = pl.multiple_of(late * HALF, HALF)
        visible = ahead >= jnp.where(s == c, 0, -HALF)
        other = jnp.where(lax.rem(s, 2) == core, 0, 1)
        k = lax.div(s, 2)
        keys = kv[other, k, pl.ds(first, HALF), :HEAD_DIM]
        values = kv[other, k, pl.ds(first, HALF), HEAD_DIM:]
        query_grad, key_grad, value_grad = tile(
            qs[late], gs[late], norm[late], delta[late], keys, values, visible
        )
        return late, (other, k), first, query_grad, jnp.concatenate([key_grad, value_grad], 1)

    def stored(late, block, first, query_grad, now):
        dq_sum[late] += query_grad
        before = dkv_ref[*block, pl.ds(first, HALF), :].astype(F32)
        dkv_ref[*block, pl.ds(first, HALF), :] = (before + now).astype(BF16)

    for first in range(0, 17, 4):
        for done in [unit(i) for i in range(first, min(first + 4, 17))]:
            stored(*done)
    mine_ref[...] = dkv_ref[0]
    yours_ref[...] = dkv_ref[1]
    for half in range(2):
        for h in range(heads):
            dq_ref[half * HALF : (half + 1) * HALF, h * HEAD_DIM : (h + 1) * HEAD_DIM] = (
                dq_sum[half, h * HALF : (h + 1) * HALF, :] * scale
            ).astype(BF16)


def late_call(q, o, g, log_norm, kv, other_kv):
    side = q.shape[1] // HEAD_DIM * HALF
    vmem = pl.BlockSpec(memory_space=pltpu.VMEM)
    stacked = jax.ShapeDtypeStruct((2, side, HEAD_DIM), BF16)
    line = jax.ShapeDtypeStruct((2, 1, side), F32)
    half = jax.ShapeDtypeStruct(kv.shape, BF16)
    return pl.pallas_call(
        late_kernel,
        out_shape=(
            stacked,
            stacked,
            line,
            line,
            jax.ShapeDtypeStruct((2, side, HEAD_DIM), F32),
            half,
            half,
        ),
        in_specs=[vmem] * 6,
        out_specs=(vmem,) * 7,
        compiler_params=pltpu.CompilerParams(vmem_limit_bytes=24 * 1024 * 1024),
        cost_estimate=pl.CostEstimate(
            flops=10**10, bytes_accessed=2**22, transcendentals=10**6
        ),
    )(q, o, g, log_norm, kv, other_kv)


def rest_call(where, kept, kv, other_kv):
    qs, gs, norm, delta, dq, dkv, other_dkv = kept
    side = qs.shape[1]
    vmem = pl.BlockSpec(memory_space=pltpu.VMEM)
    half = jax.ShapeDtypeStruct(dkv.shape, BF16)
    return pl.pallas_call(
        rest_kernel,
        out_shape=(jax.ShapeDtypeStruct((2 * HALF, side), BF16), half, half),
        in_specs=[pl.BlockSpec(memory_space=pltpu.SMEM)] + [vmem] * 9,
        out_specs=(vmem,) * 3,
        scratch_shapes=[
            pltpu.VMEM((2, side, HEAD_DIM), F32),
            pltpu.VMEM((2, *kv.shape), BF16),
            pltpu.VMEM((2, *dkv.shape), BF16),
        ],
        compiler_params=pltpu.CompilerParams(vmem_limit_bytes=24 * 1024 * 1024),
        cost_estimate=pl.CostEstimate(
            flops=10**10, bytes_accessed=2**22, transcendentals=10**6
        ),
    )(where, qs, gs, norm, delta, dq, kv, other_kv, dkv, other_dkv)


def local(q, k, v, o, log_norm, dy, w, down, up):
    ylo, x, core, yhi, z = (lax.axis_index(a) for a in CTX + TP)
    where = jnp.stack([ylo * 8 + x * 2 + core, yhi, z, core]).astype(jnp.int32)
    together = lax.optimization_barrier
    own_blocks = gathered_round(dy, "z", True)
    mixed = lax.dot_general(down, o, (((0,), (1,)), ((), ())), preferred_element_type=F32)
    mixed = jnp.concatenate([mixed[i * 16 : i * 16 + 16] for i in range(4)], 1)
    peer = turned(dy, "yhi", 1)
    other = turned(mixed.astype(BF16), "yhi", 1)
    peer = jnp.concatenate([peer, (mixed + other.astype(F32)).astype(BF16)], 1)
    kv, peer = together((jnp.concatenate([k, v], 1), peer))
    kv = lax.all_to_all(jnp.broadcast_to(kv[None], (8,) + kv.shape), CTX[:2], 0, 0)
    own_blocks, kv = together((own_blocks, kv))
    other_kv = turned(kv, "core", 1)
    own_rows, own_cots = own_call(where, own_blocks, up)
    peer_blocks = gathered_round(peer, "z", False)
    peer_rows, cots, mine, yours = adapter_call(where, peer_blocks, up, own_rows, own_cots, o)
    low = (mine + turned(yours, "core", 1).astype(F32)).astype(BF16)
    cots, low = together((cots, low))
    g = gradient_call(where, own_rows, peer_rows, w, cots, down.T)
    total = low.astype(F32) + turned(low, "ylo", 1).astype(F32)
    low, g = together((total.astype(BF16), g))
    kept = late_call(q, o, g, log_norm, kv, other_kv)
    total = low.astype(F32) + lax.ppermute(low, "x", [(i, i ^ 1) for i in range(4)]).astype(F32)
    low, kept = together((total.astype(BF16), kept))
    dq, mine, yours = rest_call(where, kept, kv, other_kv)
    total = low.astype(F32) + lax.ppermute(low, "x", [(i, 3 - i) for i in range(4)]).astype(F32)
    low, mine, yours = together((total.astype(BF16), mine, yours))
    other = turned(low, "core", 1)
    mine = (mine.astype(F32) + turned(yours, "core", 1).astype(F32)).astype(BF16)
    other, mine = together((other, mine))
    pieces = lax.all_to_all(mine, CTX[:2], 0, 0)
    first, second = jnp.where(core == 0, low, other), jnp.where(core == 0, other, low)
    cut = low.shape[1] - 256
    down_grad = jnp.concatenate([first[:, cut:], second[:, cut:]], 1).astype(F32).T
    up_total = jnp.concatenate([first[:, :cut], second[:, :cut]], 1)
    before, after = turned(up_total, "z", 1), turned(up_total, "z", -1)
    far = (turned(before[:, :cut], "z", 1), turned(after[:, cut:], "z", -1))
    up_grad = placed_round(where, [up_total, after, *far, before])
    dkv_sum, low = summed(pieces)
    other = lax.ppermute(low, "z", [(i, i ^ 1) for i in range(8)])
    dkv_sum = (dkv_sum + other.astype(F32)).astype(BF16)
    return dq, dkv_sum[:, :128], dkv_sum[:, 128:], down_grad, up_grad


def solution(mesh):
    fine = Mesh(mesh.devices.reshape(SIZES), CTX + TP)
    placed = (
        P(CTX, TP),
        P(CTX, TP),
        P(CTX, TP),
        P(CTX, TP),
        P(TP, CTX),
        P(CTX + TP, None),
        P(TP, None),
        P(TP, None),
        P(),
    )
    return jax.shard_map(
        local,
        mesh=fine,
        in_specs=placed,
        out_specs=(P(CTX, TP), P(CTX, TP), P(CTX, TP), P(TP, None), P()),
        check_vma=False,
    )
```

```python
import functools

import jax
import jax.numpy as jnp
from jax import lax
from jax.experimental import pallas as pl
from jax.experimental.pallas import tpu as pltpu
from jax.sharding import Mesh, PartitionSpec as P

CTX = ("ylo", "x", "core")
TP = ("yhi", "z")
SIZES = (2, 4, 2, 2, 8)
ADAPTER_SCALE = 2.0
LOG2E = 1.4426950408889634
F32 = jnp.float32
BF16 = jnp.bfloat16
HALF = 128
HEAD_DIM = 128
LAST = (((1,), (1,)), ((), ()))
FIRST = (((0,), (0,)), ((), ()))


def turned(x, axis, by):
    size = lax.axis_size(axis)
    return lax.ppermute(x, axis, [(i, (i + by) % size) for i in range(size)])


def rolled(x, by, axis=0):
    size = x.shape[axis]
    twice = jnp.concatenate([x, x], axis)
    return lax.dynamic_slice_in_dim(twice, by, size, axis)


def gathered_round(x, axis, far_up, before_last=lambda up, down: (up, down)):
    up, down, blocks = x, x, {0: x}
    for step in range(1, 4):
        up, down = turned(up, axis, 1), turned(down, axis, -1)
        blocks[8 - step], blocks[step] = up, down
    up, down = before_last(up, down)
    blocks[4] = turned(up, axis, 1) if far_up else turned(down, axis, -1)
    return [blocks[j] for j in range(8)]


def place_kernel(where_ref, *refs):
    blocks, out_ref = refs[:-1], refs[-1]
    width = blocks[0].shape[1]
    at = 0
    for block in blocks:
        part = lax.rem(where_ref[2] + at // width, PARTS)
        to = pl.multiple_of(part * width + at % width, 128)
        out_ref[:, pl.ds(to, block.shape[1])] = block[...]
        at += block.shape[1]


def placed_round(where, blocks):
    rows, width = blocks[0].shape
    vmem = pl.BlockSpec(memory_space=pltpu.VMEM)
    return pl.pallas_call(
        place_kernel,
        out_shape=jax.ShapeDtypeStruct((rows, width * PARTS), blocks[0].dtype),
        in_specs=[pl.BlockSpec(memory_space=pltpu.SMEM)] + [vmem] * len(blocks),
        out_specs=vmem,
        compiler_params=pltpu.CompilerParams(vmem_limit_bytes=16 * 1024 * 1024),
        cost_estimate=pl.CostEstimate(flops=0, bytes_accessed=2**20, transcendentals=0),
    )(where, *blocks)


def sum_kernel(pieces_ref, sum_ref, low_ref):
    total = pieces_ref[0].astype(F32)
    for i in range(1, pieces_ref.shape[0]):
        total += pieces_ref[i].astype(F32)
    sum_ref[...] = total
    low_ref[...] = total.astype(BF16)


def summed(pieces):
    vmem = pl.BlockSpec(memory_space=pltpu.VMEM)
    return pl.pallas_call(
        sum_kernel,
        out_shape=(
            jax.ShapeDtypeStruct(pieces.shape[1:], F32),
            jax.ShapeDtypeStruct(pieces.shape[1:], BF16),
        ),
        in_specs=[vmem],
        out_specs=(vmem, vmem),
        compiler_params=pltpu.CompilerParams(vmem_limit_bytes=16 * 1024 * 1024),
        cost_estimate=pl.CostEstimate(flops=2 * 10**10, bytes_accessed=2**21, transcendentals=0),
    )(pieces)


STEP = 1024
PARTS = 4


def row_copies(blocks, rows, sems, z):
    width = rows.shape[1]
    copies = []
    for j, block in enumerate(blocks):
        to = pl.multiple_of(lax.rem(z + j, 8) * 16, 16)
        copies.append(
            pltpu.make_async_copy(block.at[:, :width], rows.at[pl.ds(to, 16), :], sems.at[j])
        )
    return copies


def column_copies(source, to, sems):
    return [
        pltpu.make_async_copy(
            source.at[:, i * STEP : (i + 1) * STEP], to.at[:, i * STEP : (i + 1) * STEP], sems.at[i]
        )
        for i in range(source.shape[1] // STEP)
    ]


def cotangent_of(rows, up):
    cots = None
    for i in range(up.shape[1] // STEP):
        at = slice(i * STEP, (i + 1) * STEP)
        term = lax.dot_general(rows[:, at], up[:, at], LAST, preferred_element_type=F32)
        cots = term if cots is None else cots + term
    return cots.astype(BF16)


def own_kernel(where_ref, *refs):
    blocks, (up_ref, rows, cots_ref) = refs[:8], refs[8:11]
    up, row_sems, up_sems = refs[11:]
    copies = row_copies(blocks, rows, row_sems, where_ref[2]) + column_copies(up_ref, up, up_sems)
    for copy in copies:
        copy.start()
    for copy in copies:
        copy.wait()
    cots_ref[...] = cotangent_of(rows, up)


def own_call(where, blocks, up):
    vmem = pl.BlockSpec(memory_space=pltpu.VMEM)
    anywhere = pl.BlockSpec(memory_space=pl.ANY)
    rank, width = up.shape
    return pl.pallas_call(
        own_kernel,
        out_shape=(
            jax.ShapeDtypeStruct((128, width), BF16),
            jax.ShapeDtypeStruct((128, rank), BF16),
        ),
        in_specs=[pl.BlockSpec(memory_space=pltpu.SMEM)] + [anywhere] * 9,
        out_specs=(vmem,) * 2,
        scratch_shapes=[
            pltpu.VMEM((rank, width), BF16),
            pltpu.SemaphoreType.DMA((8,)),
            pltpu.SemaphoreType.DMA((width // STEP,)),
        ],
        compiler_params=pltpu.CompilerParams(vmem_limit_bytes=48 * 1024 * 1024),
        cost_estimate=pl.CostEstimate(flops=2 * 10**9, bytes_accessed=2**22, transcendentals=0),
    )(where, *blocks, up)


def adapter_kernel(where_ref, *refs):
    peer = refs[:8]
    up_ref, own_ref, own_cots_ref, o_ref, rows, cots_ref, mine_ref, yours_ref = refs[8:16]
    up, tails, chunks, row_sems, tail_sems, up_sems = refs[16:]
    yhi, z, core = where_ref[1], where_ref[2], where_ref[3]
    copies = column_copies(up_ref, up, up_sems) + row_copies(peer, rows, row_sems, z)
    copies += [
        pltpu.make_async_copy(block.at[:, rows.shape[1] :], tails.at[j], tail_sems.at[j])
        for j, block in enumerate(peer)
    ]
    for copy in copies:
        copy.start()
    wide = chunks.shape[2]
    at = pl.ds(pl.multiple_of(lax.rem(z, PARTS) * wide, wide), wide)
    chunks[yhi] = own_ref[:, at]
    for copy in copies:
        copy.wait()
    mixed = tails[0].astype(F32)
    for j in range(1, 8):
        mixed += tails[j].astype(F32)
    mixed = mixed.astype(BF16)
    mixed = jnp.concatenate([mixed[:, i * 256 : i * 256 + 256] for i in range(4)])
    chunks[1 - yhi] = rows[:, at]
    peer_cots, own_cots = cotangent_of(rows, up), own_cots_ref[...]
    cots = jnp.concatenate(
        [jnp.where(yhi == 0, own_cots, peer_cots), jnp.where(yhi == 0, peer_cots, own_cots)]
    )
    cots_ref[...] = cots
    columns = chunks[...].reshape(256, wide)
    up_part = ADAPTER_SCALE * jnp.dot(mixed, columns, preferred_element_type=F32)
    down_part = lax.dot_general(cots, o_ref[...], FIRST, preferred_element_type=F32)
    down_part = ADAPTER_SCALE * down_part
    cut = wide // 2
    first = jnp.concatenate([up_part[:, :cut], down_part[:, :256]], 1)
    second = jnp.concatenate([up_part[:, cut:], down_part[:, 256:]], 1)
    mine_ref[...] = jnp.where(core == 0, first, second)
    yours_ref[...] = jnp.where(core == 0, second, first).astype(BF16)


def adapter_call(where, peer, up, own_rows, own_cots, o):
    vmem = pl.BlockSpec(memory_space=pltpu.VMEM)
    anywhere = pl.BlockSpec(memory_space=pl.ANY)
    rank, width = up.shape
    return pl.pallas_call(
        adapter_kernel,
        out_shape=(
            jax.ShapeDtypeStruct((128, width), BF16),
            jax.ShapeDtypeStruct((256, rank), BF16),
            jax.ShapeDtypeStruct((rank, width // PARTS // 2 + 256), F32),
            jax.ShapeDtypeStruct((rank, width // PARTS // 2 + 256), BF16),
        ),
        in_specs=[pl.BlockSpec(memory_space=pltpu.SMEM)] + [anywhere] * 9 + [vmem] * 3,
        out_specs=(vmem,) * 4,
        scratch_shapes=[
            pltpu.VMEM((rank, width), BF16),
            pltpu.VMEM((8, 16, 1024), BF16),
            pltpu.VMEM((2, 128, width // PARTS), BF16),
            pltpu.SemaphoreType.DMA((8,)),
            pltpu.SemaphoreType.DMA((8,)),
            pltpu.SemaphoreType.DMA((width // STEP,)),
        ],
        compiler_params=pltpu.CompilerParams(vmem_limit_bytes=24 * 1024 * 1024),
        cost_estimate=pl.CostEstimate(flops=2 * 10**9, bytes_accessed=2**22, transcendentals=0),
    )(where, *peer, up, own_rows, own_cots, o)


def gradient_kernel(where_ref, own_ref, peer_ref, w_ref, cots_ref, down_ref, g_ref):
    yhi = where_ref[1]
    product = None
    for i in range(w_ref.shape[1] // STEP):
        at = slice(i * STEP, (i + 1) * STEP)
        rows = jnp.concatenate([own_ref[:, at], peer_ref[:, at]])
        term = lax.dot_general(rows, w_ref[:, at], LAST, preferred_element_type=F32)
        product = term if product is None else product + term
    adapter = jnp.dot(cots_ref[...], down_ref[...], preferred_element_type=F32)
    adapter = ADAPTER_SCALE * adapter
    for half in range(2):
        part = jnp.where(yhi == half, product[:128], product[128:])
        g_ref[half] = (part + adapter[half * 128 : half * 128 + 128]).astype(BF16)


def gradient_call(where, own_rows, peer_rows, w, cots, down):
    vmem = pl.BlockSpec(memory_space=pltpu.VMEM)
    return pl.pallas_call(
        gradient_kernel,
        out_shape=jax.ShapeDtypeStruct((2, 128, w.shape[0]), BF16),
        in_specs=[pl.BlockSpec(memory_space=pltpu.SMEM)] + [vmem] * 5,
        out_specs=vmem,
        compiler_params=pltpu.CompilerParams(vmem_limit_bytes=20 * 1024 * 1024),
        cost_estimate=pl.CostEstimate(flops=10**10, bytes_accessed=2**23, transcendentals=0),
    )(where, own_rows, peer_rows, w, cots, down)


def tile(q, g, norm, delta, keys, values, visible):
    scale = HEAD_DIM**-0.5
    scores = lax.dot_general(keys, q, LAST, preferred_element_type=F32)
    prob = jnp.exp2(scores * (scale * LOG2E) - norm)
    if visible is not None:
        prob = jnp.where(visible, prob, 0.0)
    prob_grad = lax.dot_general(values, g, LAST, preferred_element_type=F32)
    score_grad = (prob * (prob_grad - delta)).astype(BF16)
    value_grad = jnp.dot(prob.astype(BF16), g, preferred_element_type=F32)
    key_grad = jnp.dot(score_grad, q, preferred_element_type=F32) * scale
    query_grad = lax.dot_general(score_grad, keys, FIRST, preferred_element_type=F32)
    return query_grad, key_grad, value_grad


def late_kernel(
    q_ref, o_ref, g_ref, norm_ref, kv_ref, other_kv_ref,
    qs, gs, norm, delta, dq_sum, dkv_ref, other_dkv_ref,
):
    heads = q_ref.shape[1] // HEAD_DIM
    for half in range(2):
        rows = slice(half * HALF, (half + 1) * HALF)
        for h in range(heads):
            cols = slice(h * HEAD_DIM, (h + 1) * HEAD_DIM)
            into = slice(h * HALF, (h + 1) * HALF)
            qs[half, into, :] = q_ref[rows, cols]
            norm[half, :, into] = norm_ref[h : h + 1, rows] * LOG2E
            g = g_ref[half, :, cols]
            gs[half, into, :] = g
            product = g.astype(F32) * o_ref[rows, cols].astype(F32)
            delta[half, :, into] = jnp.sum(product.T, axis=0, keepdims=True)
    dq_sum[0] = jnp.zeros_like(dq_sum[0])
    for source, to in ((kv_ref, dkv_ref), (other_kv_ref, other_dkv_ref)):
        to[:, HALF:, :] = jnp.zeros((8, HALF, 2 * HEAD_DIM), BF16)
        for k in range(0, 8, 2):
            keys = source[k : k + 2, :HALF, :HEAD_DIM].reshape(2 * HALF, HEAD_DIM)
            values = source[k : k + 2, :HALF, HEAD_DIM:].reshape(2 * HALF, HEAD_DIM)
            query_grad, key_grad, value_grad = tile(
                qs[1], gs[1], norm[1], delta[1], keys, values, None
            )
            if k or source is not kv_ref:
                dq_sum[1] += query_grad
            else:
                dq_sum[1] = query_grad
            key_grad = key_grad.astype(BF16).reshape(2, HALF, HEAD_DIM)
            value_grad = value_grad.astype(BF16).reshape(2, HALF, HEAD_DIM)
            to[k : k + 2, :HALF, :HEAD_DIM] = key_grad
            to[k : k + 2, :HALF, HEAD_DIM:] = value_grad


def rest_kernel(
    where_ref, qs, gs, norm, delta, dq_in, kv_ref, other_kv_ref, dkv_in, other_dkv_in,
    dq_ref, mine_ref, yours_ref, dq_sum, kv, dkv_ref,
):
    c, core = where_ref[0], where_ref[3]
    heads = dq_ref.shape[1] // HEAD_DIM
    scale = HEAD_DIM**-0.5
    kv[0], kv[1] = kv_ref[...], other_kv_ref[...]
    dkv_ref[0], dkv_ref[1] = dkv_in[...], other_dkv_in[...]
    dq_sum[...] = dq_in[...]
    key_at = lax.broadcasted_iota(jnp.int32, (HALF, heads * HALF), 0)
    query_at = lax.broadcasted_iota(jnp.int32, (HALF, heads * HALF), 1) % HALF
    ahead = query_at - key_at

    def unit(i):
        late = (i > c).astype(jnp.int32)
        s = i - late
        first = pl.multiple_of(late * HALF, HALF)
        visible = ahead >= jnp.where(s == c, 0, -HALF)
        other = jnp.where(lax.rem(s, 2) == core, 0, 1)
        k = lax.div(s, 2)
        keys = kv[other, k, pl.ds(first, HALF), :HEAD_DIM]
        values = kv[other, k, pl.ds(first, HALF), HEAD_DIM:]
        query_grad, key_grad, value_grad = tile(
            qs[late], gs[late], norm[late], delta[late], keys, values, visible
        )
        return late, (other, k), first, query_grad, jnp.concatenate([key_grad, value_grad], 1)

    def stored(late, block, first, query_grad, now):
        dq_sum[late] += query_grad
        before = dkv_ref[*block, pl.ds(first, HALF), :].astype(F32)
        dkv_ref[*block, pl.ds(first, HALF), :] = (before + now).astype(BF16)

    for first in range(0, 17, 4):
        for done in [unit(i) for i in range(first, min(first + 4, 17))]:
            stored(*done)
    mine_ref[...] = dkv_ref[0]
    yours_ref[...] = dkv_ref[1]
    for half in range(2):
        for h in range(heads):
            dq_ref[half * HALF : (half + 1) * HALF, h * HEAD_DIM : (h + 1) * HEAD_DIM] = (
                dq_sum[half, h * HALF : (h + 1) * HALF, :] * scale
            ).astype(BF16)


def late_call(q, o, g, log_norm, kv, other_kv):
    side = q.shape[1] // HEAD_DIM * HALF
    vmem = pl.BlockSpec(memory_space=pltpu.VMEM)
    stacked = jax.ShapeDtypeStruct((2, side, HEAD_DIM), BF16)
    line = jax.ShapeDtypeStruct((2, 1, side), F32)
    half = jax.ShapeDtypeStruct(kv.shape, BF16)
    return pl.pallas_call(
        late_kernel,
        out_shape=(
            stacked,
            stacked,
            line,
            line,
            jax.ShapeDtypeStruct((2, side, HEAD_DIM), F32),
            half,
            half,
        ),
        in_specs=[vmem] * 6,
        out_specs=(vmem,) * 7,
        compiler_params=pltpu.CompilerParams(vmem_limit_bytes=24 * 1024 * 1024),
        cost_estimate=pl.CostEstimate(
            flops=10**10, bytes_accessed=2**22, transcendentals=10**6
        ),
    )(q, o, g, log_norm, kv, other_kv)


def rest_call(where, kept, kv, other_kv):
    qs, gs, norm, delta, dq, dkv, other_dkv = kept
    side = qs.shape[1]
    vmem = pl.BlockSpec(memory_space=pltpu.VMEM)
    half = jax.ShapeDtypeStruct(dkv.shape, BF16)
    return pl.pallas_call(
        rest_kernel,
        out_shape=(jax.ShapeDtypeStruct((2 * HALF, side), BF16), half, half),
        in_specs=[pl.BlockSpec(memory_space=pltpu.SMEM)] + [vmem] * 9,
        out_specs=(vmem,) * 3,
        scratch_shapes=[
            pltpu.VMEM((2, side, HEAD_DIM), F32),
            pltpu.VMEM((2, *kv.shape), BF16),
            pltpu.VMEM((2, *dkv.shape), BF16),
        ],
        compiler_params=pltpu.CompilerParams(vmem_limit_bytes=24 * 1024 * 1024),
        cost_estimate=pl.CostEstimate(
            flops=10**10, bytes_accessed=2**22, transcendentals=10**6
        ),
    )(where, qs, gs, norm, delta, dq, kv, other_kv, dkv, other_dkv)


def local(q, k, v, o, log_norm, dy, w, down, up):
    ylo, x, core, yhi, z = (lax.axis_index(a) for a in CTX + TP)
    where = jnp.stack([ylo * 8 + x * 2 + core, yhi, z, core]).astype(jnp.int32)
    together = lax.optimization_barrier
    own_blocks = gathered_round(dy, "z", True)
    mixed = lax.dot_general(down, o, (((0,), (1,)), ((), ())), preferred_element_type=F32)
    mixed = jnp.concatenate([mixed[i * 16 : i * 16 + 16] for i in range(4)], 1)
    peer = turned(dy, "yhi", 1)
    other = turned(mixed.astype(BF16), "yhi", 1)
    peer = jnp.concatenate([peer, (mixed + other.astype(F32)).astype(BF16)], 1)
    kv, peer = together((jnp.concatenate([k, v], 1), peer))
    kv = lax.all_to_all(jnp.broadcast_to(kv[None], (8,) + kv.shape), CTX[:2], 0, 0)
    own_blocks, kv = together((own_blocks, kv))
    other_kv = turned(kv, "core", 1)
    own_rows, own_cots = own_call(where, own_blocks, up)
    peer_blocks = gathered_round(peer, "z", False)
    peer_rows, cots, mine, yours = adapter_call(where, peer_blocks, up, own_rows, own_cots, o)
    low = (mine + turned(yours, "core", 1).astype(F32)).astype(BF16)
    cots, low = together((cots, low))
    g = gradient_call(where, own_rows, peer_rows, w, cots, down.T)
    other, g = together((turned(low, "ylo", 1), g))
    low = (low.astype(F32) + other.astype(F32)).astype(BF16)
    low, g = together((low, g))
    kept = late_call(q, o, g, log_norm, kv, other_kv)
    other = lax.ppermute(low, "x", [(i, i ^ 1) for i in range(4)])
    other, kept = together((other, kept))
    low = (low.astype(F32) + other.astype(F32)).astype(BF16)
    low, kept = together((low, kept))
    dq, mine, yours = rest_call(where, kept, kv, other_kv)
    other = lax.ppermute(low, "x", [(i, 3 - i) for i in range(4)])
    other, mine, yours = together((other, mine, yours))
    low = (low.astype(F32) + other.astype(F32)).astype(BF16)
    other = turned(low, "core", 1)
    mine = (mine.astype(F32) + turned(yours, "core", 1).astype(F32)).astype(BF16)
    other, mine = together((other, mine))
    pieces = lax.all_to_all(mine, CTX[:2], 0, 0)
    first, second = jnp.where(core == 0, low, other), jnp.where(core == 0, other, low)
    cut = low.shape[1] - 256
    down_grad = jnp.concatenate([first[:, cut:], second[:, cut:]], 1).astype(F32).T
    up_total = jnp.concatenate([first[:, :cut], second[:, :cut]], 1)
    before, after = turned(up_total, "z", 1), turned(up_total, "z", -1)
    far = (turned(before[:, :cut], "z", 1), turned(after[:, cut:], "z", -1))
    up_grad = placed_round(where, [up_total, after, *far, before])
    dkv_sum, low = summed(pieces)
    other = lax.ppermute(low, "z", [(i, i ^ 1) for i in range(8)])
    dkv_sum = (dkv_sum + other.astype(F32)).astype(BF16)
    return dq, dkv_sum[:, :128], dkv_sum[:, 128:], down_grad, up_grad


def solution(mesh):
    fine = Mesh(mesh.devices.reshape(SIZES), CTX + TP)
    placed = (
        P(CTX, TP),
        P(CTX, TP),
        P(CTX, TP),
        P(CTX, TP),
        P(TP, CTX),
        P(CTX + TP, None),
        P(TP, None),
        P(TP, None),
        P(),
    )
    return jax.shard_map(
        local,
        mesh=fine,
        in_specs=placed,
        out_specs=(P(CTX, TP), P(CTX, TP), P(CTX, TP), P(TP, None), P()),
        check_vma=False,
    )
```

```python
import functools

import jax
import jax.numpy as jnp
from jax import lax
from jax.experimental import pallas as pl
from jax.experimental.pallas import tpu as pltpu
from jax.sharding import Mesh, PartitionSpec as P

CTX = ("ylo", "x", "core")
TP = ("yhi", "z")
SIZES = (2, 4, 2, 2, 8)
ADAPTER_SCALE = 2.0
LOG2E = 1.4426950408889634
F32 = jnp.float32
BF16 = jnp.bfloat16
HALF = 128
HEAD_DIM = 128
LAST = (((1,), (1,)), ((), ()))
FIRST = (((0,), (0,)), ((), ()))


def turned(x, axis, by):
    size = lax.axis_size(axis)
    return lax.ppermute(x, axis, [(i, (i + by) % size) for i in range(size)])


def rolled(x, by, axis=0):
    size = x.shape[axis]
    twice = jnp.concatenate([x, x], axis)
    return lax.dynamic_slice_in_dim(twice, by, size, axis)


def gathered_round(x, axis, far_up, before_last=lambda up, down: (up, down)):
    up, down, blocks = x, x, {0: x}
    for step in range(1, 4):
        up, down = turned(up, axis, 1), turned(down, axis, -1)
        blocks[8 - step], blocks[step] = up, down
    up, down = before_last(up, down)
    blocks[4] = turned(up, axis, 1) if far_up else turned(down, axis, -1)
    return [blocks[j] for j in range(8)]


def place_kernel(where_ref, *refs):
    blocks, out_ref = refs[:-1], refs[-1]
    width = blocks[0].shape[1]
    at = 0
    for block in blocks:
        part = lax.rem(where_ref[2] + at // width, PARTS)
        to = pl.multiple_of(part * width + at % width, 128)
        out_ref[:, pl.ds(to, block.shape[1])] = block[...]
        at += block.shape[1]


def placed_round(where, blocks):
    rows, width = blocks[0].shape
    vmem = pl.BlockSpec(memory_space=pltpu.VMEM)
    return pl.pallas_call(
        place_kernel,
        out_shape=jax.ShapeDtypeStruct((rows, width * PARTS), blocks[0].dtype),
        in_specs=[pl.BlockSpec(memory_space=pltpu.SMEM)] + [vmem] * len(blocks),
        out_specs=vmem,
        compiler_params=pltpu.CompilerParams(vmem_limit_bytes=16 * 1024 * 1024),
        cost_estimate=pl.CostEstimate(flops=0, bytes_accessed=2**20, transcendentals=0),
    )(where, *blocks)


def sum_kernel(pieces_ref, sum_ref, low_ref):
    total = pieces_ref[0].astype(F32)
    for i in range(1, pieces_ref.shape[0]):
        total += pieces_ref[i].astype(F32)
    sum_ref[...] = total
    low_ref[...] = total.astype(BF16)


def summed(pieces):
    vmem = pl.BlockSpec(memory_space=pltpu.VMEM)
    return pl.pallas_call(
        sum_kernel,
        out_shape=(
            jax.ShapeDtypeStruct(pieces.shape[1:], F32),
            jax.ShapeDtypeStruct(pieces.shape[1:], BF16),
        ),
        in_specs=[vmem],
        out_specs=(vmem, vmem),
        compiler_params=pltpu.CompilerParams(vmem_limit_bytes=16 * 1024 * 1024),
        cost_estimate=pl.CostEstimate(flops=2 * 10**10, bytes_accessed=2**21, transcendentals=0),
    )(pieces)


STEP = 1024
PARTS = 4


def row_copies(blocks, rows, sems, z):
    width = rows.shape[1]
    copies = []
    for j, block in enumerate(blocks):
        to = pl.multiple_of(lax.rem(z + j, 8) * 16, 16)
        copies.append(
            pltpu.make_async_copy(block.at[:, :width], rows.at[pl.ds(to, 16), :], sems.at[j])
        )
    return copies


def column_copies(source, to, sems):
    return [
        pltpu.make_async_copy(
            source.at[:, i * STEP : (i + 1) * STEP], to.at[:, i * STEP : (i + 1) * STEP], sems.at[i]
        )
        for i in range(source.shape[1] // STEP)
    ]


def cotangent_of(rows, up):
    cots = None
    for i in range(up.shape[1] // STEP):
        at = slice(i * STEP, (i + 1) * STEP)
        term = lax.dot_general(rows[:, at], up[:, at], LAST, preferred_element_type=F32)
        cots = term if cots is None else cots + term
    return cots.astype(BF16)


def own_kernel(where_ref, *refs):
    blocks, (up_ref, rows, cots_ref) = refs[:8], refs[8:11]
    up, row_sems, up_sems = refs[11:]
    copies = row_copies(blocks, rows, row_sems, where_ref[2]) + column_copies(up_ref, up, up_sems)
    for copy in copies:
        copy.start()
    for copy in copies:
        copy.wait()
    cots_ref[...] = cotangent_of(rows, up)


def own_call(where, blocks, up):
    vmem = pl.BlockSpec(memory_space=pltpu.VMEM)
    anywhere = pl.BlockSpec(memory_space=pl.ANY)
    rank, width = up.shape
    return pl.pallas_call(
        own_kernel,
        out_shape=(
            jax.ShapeDtypeStruct((128, width), BF16),
            jax.ShapeDtypeStruct((128, rank), BF16),
        ),
        in_specs=[pl.BlockSpec(memory_space=pltpu.SMEM)] + [anywhere] * 9,
        out_specs=(vmem,) * 2,
        scratch_shapes=[
            pltpu.VMEM((rank, width), BF16),
            pltpu.SemaphoreType.DMA((8,)),
            pltpu.SemaphoreType.DMA((width // STEP,)),
        ],
        compiler_params=pltpu.CompilerParams(vmem_limit_bytes=48 * 1024 * 1024),
        cost_estimate=pl.CostEstimate(flops=2 * 10**9, bytes_accessed=2**22, transcendentals=0),
    )(where, *blocks, up)


def adapter_kernel(where_ref, *refs):
    peer = refs[:8]
    up_ref, own_ref, own_cots_ref, o_ref, rows, cots_ref, mine_ref, yours_ref = refs[8:16]
    up, tails, chunks, row_sems, tail_sems, up_sems = refs[16:]
    yhi, z, core = where_ref[1], where_ref[2], where_ref[3]
    copies = column_copies(up_ref, up, up_sems) + row_copies(peer, rows, row_sems, z)
    copies += [
        pltpu.make_async_copy(block.at[:, rows.shape[1] :], tails.at[j], tail_sems.at[j])
        for j, block in enumerate(peer)
    ]
    for copy in copies:
        copy.start()
    wide = chunks.shape[2]
    at = pl.ds(pl.multiple_of(lax.rem(z, PARTS) * wide, wide), wide)
    chunks[yhi] = own_ref[:, at]
    for copy in copies:
        copy.wait()
    mixed = tails[0].astype(F32)
    for j in range(1, 8):
        mixed += tails[j].astype(F32)
    mixed = mixed.astype(BF16)
    mixed = jnp.concatenate([mixed[:, i * 256 : i * 256 + 256] for i in range(4)])
    chunks[1 - yhi] = rows[:, at]
    peer_cots, own_cots = cotangent_of(rows, up), own_cots_ref[...]
    cots = jnp.concatenate(
        [jnp.where(yhi == 0, own_cots, peer_cots), jnp.where(yhi == 0, peer_cots, own_cots)]
    )
    cots_ref[...] = cots
    columns = chunks[...].reshape(256, wide)
    up_part = ADAPTER_SCALE * jnp.dot(mixed, columns, preferred_element_type=F32)
    down_part = lax.dot_general(cots, o_ref[...], FIRST, preferred_element_type=F32)
    down_part = ADAPTER_SCALE * down_part
    cut = wide // 2
    first = jnp.concatenate([up_part[:, :cut], down_part[:, :256]], 1)
    second = jnp.concatenate([up_part[:, cut:], down_part[:, 256:]], 1)
    mine_ref[...] = jnp.where(core == 0, first, second)
    yours_ref[...] = jnp.where(core == 0, second, first).astype(BF16)


def adapter_call(where, peer, up, own_rows, own_cots, o):
    vmem = pl.BlockSpec(memory_space=pltpu.VMEM)
    anywhere = pl.BlockSpec(memory_space=pl.ANY)
    rank, width = up.shape
    return pl.pallas_call(
        adapter_kernel,
        out_shape=(
            jax.ShapeDtypeStruct((128, width), BF16),
            jax.ShapeDtypeStruct((256, rank), BF16),
            jax.ShapeDtypeStruct((rank, width // PARTS // 2 + 256), F32),
            jax.ShapeDtypeStruct((rank, width // PARTS // 2 + 256), BF16),
        ),
        in_specs=[pl.BlockSpec(memory_space=pltpu.SMEM)] + [anywhere] * 9 + [vmem] * 3,
        out_specs=(vmem,) * 4,
        scratch_shapes=[
            pltpu.VMEM((rank, width), BF16),
            pltpu.VMEM((8, 16, 1024), BF16),
            pltpu.VMEM((2, 128, width // PARTS), BF16),
            pltpu.SemaphoreType.DMA((8,)),
            pltpu.SemaphoreType.DMA((8,)),
            pltpu.SemaphoreType.DMA((width // STEP,)),
        ],
        compiler_params=pltpu.CompilerParams(vmem_limit_bytes=24 * 1024 * 1024),
        cost_estimate=pl.CostEstimate(flops=2 * 10**9, bytes_accessed=2**22, transcendentals=0),
    )(where, *peer, up, own_rows, own_cots, o)


def gradient_kernel(where_ref, own_ref, peer_ref, w_ref, cots_ref, down_ref, g_ref):
    yhi = where_ref[1]
    product = None
    for i in range(w_ref.shape[1] // STEP):
        at = slice(i * STEP, (i + 1) * STEP)
        rows = jnp.concatenate([own_ref[:, at], peer_ref[:, at]])
        term = lax.dot_general(rows, w_ref[:, at], LAST, preferred_element_type=F32)
        product = term if product is None else product + term
    adapter = jnp.dot(cots_ref[...], down_ref[...], preferred_element_type=F32)
    adapter = ADAPTER_SCALE * adapter
    for half in range(2):
        part = jnp.where(yhi == half, product[:128], product[128:])
        g_ref[half] = (part + adapter[half * 128 : half * 128 + 128]).astype(BF16)


def gradient_call(where, own_rows, peer_rows, w, cots, down):
    vmem = pl.BlockSpec(memory_space=pltpu.VMEM)
    return pl.pallas_call(
        gradient_kernel,
        out_shape=jax.ShapeDtypeStruct((2, 128, w.shape[0]), BF16),
        in_specs=[pl.BlockSpec(memory_space=pltpu.SMEM)] + [vmem] * 5,
        out_specs=vmem,
        compiler_params=pltpu.CompilerParams(vmem_limit_bytes=20 * 1024 * 1024),
        cost_estimate=pl.CostEstimate(flops=10**10, bytes_accessed=2**23, transcendentals=0),
    )(where, own_rows, peer_rows, w, cots, down)


def tile(q, g, norm, delta, keys, values, visible):
    scale = HEAD_DIM**-0.5
    scores = lax.dot_general(keys, q, LAST, preferred_element_type=F32)
    prob = jnp.exp2(scores * (scale * LOG2E) - norm)
    if visible is not None:
        prob = jnp.where(visible, prob, 0.0)
    prob_grad = lax.dot_general(values, g, LAST, preferred_element_type=F32)
    score_grad = (prob * (prob_grad - delta)).astype(BF16)
    value_grad = jnp.dot(prob.astype(BF16), g, preferred_element_type=F32)
    key_grad = jnp.dot(score_grad, q, preferred_element_type=F32) * scale
    query_grad = lax.dot_general(score_grad, keys, FIRST, preferred_element_type=F32)
    return query_grad, key_grad, value_grad


def late_kernel(
    q_ref, o_ref, g_ref, norm_ref, kv_ref, other_kv_ref,
    qs, gs, norm, delta, dq_sum, dkv_ref, other_dkv_ref,
):
    heads = q_ref.shape[1] // HEAD_DIM
    for half in range(2):
        rows = slice(half * HALF, (half + 1) * HALF)
        for h in range(heads):
            cols = slice(h * HEAD_DIM, (h + 1) * HEAD_DIM)
            into = slice(h * HALF, (h + 1) * HALF)
            qs[half, into, :] = q_ref[rows, cols]
            norm[half, :, into] = norm_ref[h : h + 1, rows] * LOG2E
            g = g_ref[half, :, cols]
            gs[half, into, :] = g
            product = g.astype(F32) * o_ref[rows, cols].astype(F32)
            delta[half, :, into] = jnp.sum(product.T, axis=0, keepdims=True)
    dq_sum[0] = jnp.zeros_like(dq_sum[0])
    for source, to in ((kv_ref, dkv_ref), (other_kv_ref, other_dkv_ref)):
        to[:, HALF:, :] = jnp.zeros((8, HALF, 2 * HEAD_DIM), BF16)
        for k in range(0, 8, 2):
            keys = source[k : k + 2, :HALF, :HEAD_DIM].reshape(2 * HALF, HEAD_DIM)
            values = source[k : k + 2, :HALF, HEAD_DIM:].reshape(2 * HALF, HEAD_DIM)
            query_grad, key_grad, value_grad = tile(
                qs[1], gs[1], norm[1], delta[1], keys, values, None
            )
            if k or source is not kv_ref:
                dq_sum[1] += query_grad
            else:
                dq_sum[1] = query_grad
            key_grad = key_grad.astype(BF16).reshape(2, HALF, HEAD_DIM)
            value_grad = value_grad.astype(BF16).reshape(2, HALF, HEAD_DIM)
            to[k : k + 2, :HALF, :HEAD_DIM] = key_grad
            to[k : k + 2, :HALF, HEAD_DIM:] = value_grad


def rest_kernel(
    where_ref, qs, gs, norm, delta, dq_in, kv_ref, other_kv_ref, dkv_in, other_dkv_in,
    dq_ref, mine_ref, yours_ref, dq_sum, kv, dkv_ref,
):
    c, core = where_ref[0], where_ref[3]
    heads = dq_ref.shape[1] // HEAD_DIM
    scale = HEAD_DIM**-0.5
    kv[0], kv[1] = kv_ref[...], other_kv_ref[...]
    dkv_ref[0], dkv_ref[1] = dkv_in[...], other_dkv_in[...]
    dq_sum[...] = dq_in[...]
    side = (2 * HALF, heads * HALF)
    key_at = lax.broadcasted_iota(jnp.int32, side, 0)
    query_at = lax.broadcasted_iota(jnp.int32, side, 1) % HALF
    ahead = query_at - key_at % HALF
    second = key_at >= HALF

    def unit(i):
        late = (i > lax.div(c, 2)).astype(jnp.int32)
        k = i - late
        first = pl.multiple_of(late * HALF, HALF)
        behind = [
            jnp.where(s == c, 0, jnp.where((s < c) == (late == 0), -HALF, HALF))
            for s in (2 * k + core, 2 * k + 1 - core)
        ]
        visible = ahead >= jnp.where(second, behind[1], behind[0])
        keys = kv[:, k, pl.ds(first, HALF), :HEAD_DIM].reshape(2 * HALF, HEAD_DIM)
        values = kv[:, k, pl.ds(first, HALF), HEAD_DIM:].reshape(2 * HALF, HEAD_DIM)
        query_grad, key_grad, value_grad = tile(
            qs[late], gs[late], norm[late], delta[late], keys, values, visible
        )
        return late, k, first, query_grad, jnp.concatenate([key_grad, value_grad], 1)

    def stored(late, k, first, query_grad, now):
        dq_sum[late] += query_grad
        at = (slice(None), k, pl.ds(first, HALF), slice(None))
        before = dkv_ref[at].astype(F32).reshape(now.shape)
        dkv_ref[at] = (before + now).astype(BF16).reshape(2, HALF, now.shape[1])

    for first in range(0, 9, 3):
        for done in [unit(i) for i in range(first, first + 3)]:
            stored(*done)
    mine_ref[...] = dkv_ref[0]
    yours_ref[...] = dkv_ref[1]
    for half in range(2):
        for h in range(heads):
            dq_ref[half * HALF : (half + 1) * HALF, h * HEAD_DIM : (h + 1) * HEAD_DIM] = (
                dq_sum[half, h * HALF : (h + 1) * HALF, :] * scale
            ).astype(BF16)


def late_call(q, o, g, log_norm, kv, other_kv):
    side = q.shape[1] // HEAD_DIM * HALF
    vmem = pl.BlockSpec(memory_space=pltpu.VMEM)
    stacked = jax.ShapeDtypeStruct((2, side, HEAD_DIM), BF16)
    line = jax.ShapeDtypeStruct((2, 1, side), F32)
    half = jax.ShapeDtypeStruct(kv.shape, BF16)
    return pl.pallas_call(
        late_kernel,
        out_shape=(
            stacked,
            stacked,
            line,
            line,
            jax.ShapeDtypeStruct((2, side, HEAD_DIM), F32),
            half,
            half,
        ),
        in_specs=[vmem] * 6,
        out_specs=(vmem,) * 7,
        compiler_params=pltpu.CompilerParams(vmem_limit_bytes=24 * 1024 * 1024),
        cost_estimate=pl.CostEstimate(
            flops=10**10, bytes_accessed=2**22, transcendentals=10**6
        ),
    )(q, o, g, log_norm, kv, other_kv)


def rest_call(where, kept, kv, other_kv):
    qs, gs, norm, delta, dq, dkv, other_dkv = kept
    side = qs.shape[1]
    vmem = pl.BlockSpec(memory_space=pltpu.VMEM)
    half = jax.ShapeDtypeStruct(dkv.shape, BF16)
    return pl.pallas_call(
        rest_kernel,
        out_shape=(jax.ShapeDtypeStruct((2 * HALF, side), BF16), half, half),
        in_specs=[pl.BlockSpec(memory_space=pltpu.SMEM)] + [vmem] * 9,
        out_specs=(vmem,) * 3,
        scratch_shapes=[
            pltpu.VMEM((2, side, HEAD_DIM), F32),
            pltpu.VMEM((2, *kv.shape), BF16),
            pltpu.VMEM((2, *dkv.shape), BF16),
        ],
        compiler_params=pltpu.CompilerParams(vmem_limit_bytes=24 * 1024 * 1024),
        cost_estimate=pl.CostEstimate(
            flops=10**10, bytes_accessed=2**22, transcendentals=10**6
        ),
    )(where, qs, gs, norm, delta, dq, kv, other_kv, dkv, other_dkv)


def local(q, k, v, o, log_norm, dy, w, down, up):
    ylo, x, core, yhi, z = (lax.axis_index(a) for a in CTX + TP)
    where = jnp.stack([ylo * 8 + x * 2 + core, yhi, z, core]).astype(jnp.int32)
    together = lax.optimization_barrier
    own_blocks = gathered_round(dy, "z", True)
    mixed = lax.dot_general(down, o, (((0,), (1,)), ((), ())), preferred_element_type=F32)
    mixed = jnp.concatenate([mixed[i * 16 : i * 16 + 16] for i in range(4)], 1)
    peer = turned(dy, "yhi", 1)
    other = turned(mixed.astype(BF16), "yhi", 1)
    peer = jnp.concatenate([peer, (mixed + other.astype(F32)).astype(BF16)], 1)
    kv, peer = together((jnp.concatenate([k, v], 1), peer))
    kv = lax.all_to_all(jnp.broadcast_to(kv[None], (8,) + kv.shape), CTX[:2], 0, 0)
    own_blocks, kv = together((own_blocks, kv))
    other_kv = turned(kv, "core", 1)
    own_rows, own_cots = own_call(where, own_blocks, up)
    peer_blocks = gathered_round(peer, "z", False)
    peer_rows, cots, mine, yours = adapter_call(where, peer_blocks, up, own_rows, own_cots, o)
    low = (mine + turned(yours, "core", 1).astype(F32)).astype(BF16)
    cots, low = together((cots, low))
    g = gradient_call(where, own_rows, peer_rows, w, cots, down.T)
    other, g = together((turned(low, "ylo", 1), g))
    low = (low.astype(F32) + other.astype(F32)).astype(BF16)
    low, g = together((low, g))
    kept = late_call(q, o, g, log_norm, kv, other_kv)
    other = lax.ppermute(low, "x", [(i, i ^ 1) for i in range(4)])
    other, kept = together((other, kept))
    low = (low.astype(F32) + other.astype(F32)).astype(BF16)
    low, kept = together((low, kept))
    dq, mine, yours = rest_call(where, kept, kv, other_kv)
    other = lax.ppermute(low, "x", [(i, 3 - i) for i in range(4)])
    other, mine, yours = together((other, mine, yours))
    low = (low.astype(F32) + other.astype(F32)).astype(BF16)
    other = turned(low, "core", 1)
    mine = (mine.astype(F32) + turned(yours, "core", 1).astype(F32)).astype(BF16)
    other, mine = together((other, mine))
    pieces = lax.all_to_all(mine, CTX[:2], 0, 0)
    first, second = jnp.where(core == 0, low, other), jnp.where(core == 0, other, low)
    cut = low.shape[1] - 256
    down_grad = jnp.concatenate([first[:, cut:], second[:, cut:]], 1).astype(F32).T
    up_total = jnp.concatenate([first[:, :cut], second[:, :cut]], 1)
    before, after = turned(up_total, "z", 1), turned(up_total, "z", -1)
    far = (turned(before[:, :cut], "z", 1), turned(after[:, cut:], "z", -1))
    up_grad = placed_round(where, [up_total, after, *far, before])
    dkv_sum, low = summed(pieces)
    other = lax.ppermute(low, "z", [(i, i ^ 1) for i in range(8)])
    dkv_sum = (dkv_sum + other.astype(F32)).astype(BF16)
    return dq, dkv_sum[:, :128], dkv_sum[:, 128:], down_grad, up_grad


def solution(mesh):
    fine = Mesh(mesh.devices.reshape(SIZES), CTX + TP)
    placed = (
        P(CTX, TP),
        P(CTX, TP),
        P(CTX, TP),
        P(CTX, TP),
        P(TP, CTX),
        P(CTX + TP, None),
        P(TP, None),
        P(TP, None),
        P(),
    )
    return jax.shard_map(
        local,
        mesh=fine,
        in_specs=placed,
        out_specs=(P(CTX, TP), P(CTX, TP), P(CTX, TP), P(TP, None), P()),
        check_vma=False,
    )
```

```python
import functools

import jax
import jax.numpy as jnp
from jax import lax
from jax.experimental import pallas as pl
from jax.experimental.pallas import tpu as pltpu
from jax.sharding import Mesh, PartitionSpec as P

CTX = ("ylo", "x", "core")
TP = ("yhi", "z")
SIZES = (2, 4, 2, 2, 8)
ADAPTER_SCALE = 2.0
LOG2E = 1.4426950408889634
F32 = jnp.float32
BF16 = jnp.bfloat16
HALF = 128
HEAD_DIM = 128
LAST = (((1,), (1,)), ((), ()))
FIRST = (((0,), (0,)), ((), ()))


def turned(x, axis, by):
    size = lax.axis_size(axis)
    return lax.ppermute(x, axis, [(i, (i + by) % size) for i in range(size)])


def rolled(x, by, axis=0):
    size = x.shape[axis]
    twice = jnp.concatenate([x, x], axis)
    return lax.dynamic_slice_in_dim(twice, by, size, axis)


def gathered_round(x, axis, far_up, before_last=lambda up, down: (up, down)):
    up, down, blocks = x, x, {0: x}
    for step in range(1, 4):
        up, down = turned(up, axis, 1), turned(down, axis, -1)
        blocks[8 - step], blocks[step] = up, down
    up, down = before_last(up, down)
    blocks[4] = turned(up, axis, 1) if far_up else turned(down, axis, -1)
    return [blocks[j] for j in range(8)]


def place_kernel(where_ref, *refs):
    blocks, out_ref = refs[:-1], refs[-1]
    width = blocks[0].shape[1]
    at = 0
    for block in blocks:
        part = lax.rem(where_ref[2] + at // width, PARTS)
        to = pl.multiple_of(part * width + at % width, 128)
        out_ref[:, pl.ds(to, block.shape[1])] = block[...]
        at += block.shape[1]


def placed_round(where, blocks):
    rows, width = blocks[0].shape
    vmem = pl.BlockSpec(memory_space=pltpu.VMEM)
    return pl.pallas_call(
        place_kernel,
        out_shape=jax.ShapeDtypeStruct((rows, width * PARTS), blocks[0].dtype),
        in_specs=[pl.BlockSpec(memory_space=pltpu.SMEM)] + [vmem] * len(blocks),
        out_specs=vmem,
        compiler_params=pltpu.CompilerParams(vmem_limit_bytes=16 * 1024 * 1024),
        cost_estimate=pl.CostEstimate(flops=0, bytes_accessed=2**20, transcendentals=0),
    )(where, *blocks)


def sum_kernel(pieces_ref, sum_ref, low_ref):
    total = pieces_ref[0].astype(F32)
    for i in range(1, pieces_ref.shape[0]):
        total += pieces_ref[i].astype(F32)
    sum_ref[...] = total
    low_ref[...] = total.astype(BF16)


def summed(pieces):
    vmem = pl.BlockSpec(memory_space=pltpu.VMEM)
    return pl.pallas_call(
        sum_kernel,
        out_shape=(
            jax.ShapeDtypeStruct(pieces.shape[1:], F32),
            jax.ShapeDtypeStruct(pieces.shape[1:], BF16),
        ),
        in_specs=[vmem],
        out_specs=(vmem, vmem),
        compiler_params=pltpu.CompilerParams(vmem_limit_bytes=16 * 1024 * 1024),
        cost_estimate=pl.CostEstimate(flops=2 * 10**10, bytes_accessed=2**21, transcendentals=0),
    )(pieces)


STEP = 1024
PARTS = 4


def row_copies(blocks, rows, sems, z):
    width = rows.shape[1]
    copies = []
    for j, block in enumerate(blocks):
        to = pl.multiple_of(lax.rem(z + j, 8) * 16, 16)
        copies.append(
            pltpu.make_async_copy(block.at[:, :width], rows.at[pl.ds(to, 16), :], sems.at[j])
        )
    return copies


def column_copies(source, to, sems):
    return [
        pltpu.make_async_copy(
            source.at[:, i * STEP : (i + 1) * STEP], to.at[:, i * STEP : (i + 1) * STEP], sems.at[i]
        )
        for i in range(source.shape[1] // STEP)
    ]


def cotangent_of(rows, up):
    cots = None
    for i in range(up.shape[1] // STEP):
        at = slice(i * STEP, (i + 1) * STEP)
        term = lax.dot_general(rows[:, at], up[:, at], LAST, preferred_element_type=F32)
        cots = term if cots is None else cots + term
    return cots.astype(BF16)


def own_kernel(where_ref, *refs):
    blocks, (up_ref, rows, cots_ref) = refs[:8], refs[8:11]
    up, row_sems, up_sems = refs[11:]
    copies = row_copies(blocks, rows, row_sems, where_ref[2]) + column_copies(up_ref, up, up_sems)
    for copy in copies:
        copy.start()
    for copy in copies:
        copy.wait()
    cots_ref[...] = cotangent_of(rows, up)


def own_call(where, blocks, up):
    vmem = pl.BlockSpec(memory_space=pltpu.VMEM)
    anywhere = pl.BlockSpec(memory_space=pl.ANY)
    rank, width = up.shape
    return pl.pallas_call(
        own_kernel,
        out_shape=(
            jax.ShapeDtypeStruct((128, width), BF16),
            jax.ShapeDtypeStruct((128, rank), BF16),
        ),
        in_specs=[pl.BlockSpec(memory_space=pltpu.SMEM)] + [anywhere] * 9,
        out_specs=(vmem,) * 2,
        scratch_shapes=[
            pltpu.VMEM((rank, width), BF16),
            pltpu.SemaphoreType.DMA((8,)),
            pltpu.SemaphoreType.DMA((width // STEP,)),
        ],
        compiler_params=pltpu.CompilerParams(vmem_limit_bytes=48 * 1024 * 1024),
        cost_estimate=pl.CostEstimate(flops=2 * 10**9, bytes_accessed=2**22, transcendentals=0),
    )(where, *blocks, up)


def adapter_kernel(where_ref, *refs):
    peer = refs[:8]
    up_ref, own_ref, own_cots_ref, o_ref, rows, cots_ref, mine_ref, yours_ref = refs[8:16]
    up, tails, chunks, row_sems, tail_sems, up_sems = refs[16:]
    yhi, z, core = where_ref[1], where_ref[2], where_ref[3]
    copies = column_copies(up_ref, up, up_sems) + row_copies(peer, rows, row_sems, z)
    copies += [
        pltpu.make_async_copy(block.at[:, rows.shape[1] :], tails.at[j], tail_sems.at[j])
        for j, block in enumerate(peer)
    ]
    for copy in copies:
        copy.start()
    wide = chunks.shape[2]
    at = pl.ds(pl.multiple_of(lax.rem(z, PARTS) * wide, wide), wide)
    chunks[yhi] = own_ref[:, at]
    for copy in copies:
        copy.wait()
    mixed = tails[0].astype(F32)
    for j in range(1, 8):
        mixed += tails[j].astype(F32)
    mixed = mixed.astype(BF16)
    mixed = jnp.concatenate([mixed[:, i * 256 : i * 256 + 256] for i in range(4)])
    chunks[1 - yhi] = rows[:, at]
    peer_cots, own_cots = cotangent_of(rows, up), own_cots_ref[...]
    cots = jnp.concatenate(
        [jnp.where(yhi == 0, own_cots, peer_cots), jnp.where(yhi == 0, peer_cots, own_cots)]
    )
    cots_ref[...] = cots
    columns = chunks[...].reshape(256, wide)
    up_part = ADAPTER_SCALE * jnp.dot(mixed, columns, preferred_element_type=F32)
    down_part = lax.dot_general(cots, o_ref[...], FIRST, preferred_element_type=F32)
    down_part = ADAPTER_SCALE * down_part
    cut = wide // 2
    first = jnp.concatenate([up_part[:, :cut], down_part[:, :256]], 1)
    second = jnp.concatenate([up_part[:, cut:], down_part[:, 256:]], 1)
    mine_ref[...] = jnp.where(core == 0, first, second)
    yours_ref[...] = jnp.where(core == 0, second, first).astype(BF16)


def adapter_call(where, peer, up, own_rows, own_cots, o):
    vmem = pl.BlockSpec(memory_space=pltpu.VMEM)
    anywhere = pl.BlockSpec(memory_space=pl.ANY)
    rank, width = up.shape
    return pl.pallas_call(
        adapter_kernel,
        out_shape=(
            jax.ShapeDtypeStruct((128, width), BF16),
            jax.ShapeDtypeStruct((256, rank), BF16),
            jax.ShapeDtypeStruct((rank, width // PARTS // 2 + 256), F32),
            jax.ShapeDtypeStruct((rank, width // PARTS // 2 + 256), BF16),
        ),
        in_specs=[pl.BlockSpec(memory_space=pltpu.SMEM)] + [anywhere] * 9 + [vmem] * 3,
        out_specs=(vmem,) * 4,
        scratch_shapes=[
            pltpu.VMEM((rank, width), BF16),
            pltpu.VMEM((8, 16, 1024), BF16),
            pltpu.VMEM((2, 128, width // PARTS), BF16),
            pltpu.SemaphoreType.DMA((8,)),
            pltpu.SemaphoreType.DMA((8,)),
            pltpu.SemaphoreType.DMA((width // STEP,)),
        ],
        compiler_params=pltpu.CompilerParams(vmem_limit_bytes=24 * 1024 * 1024),
        cost_estimate=pl.CostEstimate(flops=2 * 10**9, bytes_accessed=2**22, transcendentals=0),
    )(where, *peer, up, own_rows, own_cots, o)


def gradient_kernel(where_ref, own_ref, peer_ref, w_ref, cots_ref, down_ref, g_ref):
    yhi = where_ref[1]
    product = None
    for i in range(w_ref.shape[1] // STEP):
        at = slice(i * STEP, (i + 1) * STEP)
        rows = jnp.concatenate([own_ref[:, at], peer_ref[:, at]])
        term = lax.dot_general(rows, w_ref[:, at], LAST, preferred_element_type=F32)
        product = term if product is None else product + term
    adapter = jnp.dot(cots_ref[...], down_ref[...], preferred_element_type=F32)
    adapter = ADAPTER_SCALE * adapter
    for half in range(2):
        part = jnp.where(yhi == half, product[:128], product[128:])
        g_ref[half] = (part + adapter[half * 128 : half * 128 + 128]).astype(BF16)


def gradient_call(where, own_rows, peer_rows, w, cots, down):
    vmem = pl.BlockSpec(memory_space=pltpu.VMEM)
    return pl.pallas_call(
        gradient_kernel,
        out_shape=jax.ShapeDtypeStruct((2, 128, w.shape[0]), BF16),
        in_specs=[pl.BlockSpec(memory_space=pltpu.SMEM)] + [vmem] * 5,
        out_specs=vmem,
        compiler_params=pltpu.CompilerParams(vmem_limit_bytes=20 * 1024 * 1024),
        cost_estimate=pl.CostEstimate(flops=10**10, bytes_accessed=2**23, transcendentals=0),
    )(where, own_rows, peer_rows, w, cots, down)


def tile(q, g, norm, delta, keys, values, visible):
    scale = HEAD_DIM**-0.5
    scores = lax.dot_general(keys, q, LAST, preferred_element_type=F32)
    prob = jnp.exp2(scores * (scale * LOG2E) - norm)
    if visible is not None:
        prob = jnp.where(visible, prob, 0.0)
    prob_grad = lax.dot_general(values, g, LAST, preferred_element_type=F32)
    score_grad = (prob * (prob_grad - delta)).astype(BF16)
    value_grad = jnp.dot(prob.astype(BF16), g, preferred_element_type=F32)
    key_grad = jnp.dot(score_grad, q, preferred_element_type=F32) * scale
    query_grad = lax.dot_general(score_grad, keys, FIRST, preferred_element_type=F32)
    return query_grad, key_grad, value_grad


def late_kernel(
    q_ref, o_ref, g_ref, norm_ref, kv_ref, other_kv_ref,
    qs, gs, norm, delta, dq_sum, dkv_ref, other_dkv_ref,
):
    heads = q_ref.shape[1] // HEAD_DIM
    for half in range(2):
        rows = slice(half * HALF, (half + 1) * HALF)
        for h in range(heads):
            cols = slice(h * HEAD_DIM, (h + 1) * HEAD_DIM)
            into = slice(h * HALF, (h + 1) * HALF)
            qs[half, into, :] = q_ref[rows, cols]
            norm[half, :, into] = norm_ref[h : h + 1, rows] * LOG2E
            g = g_ref[half, :, cols]
            gs[half, into, :] = g
            product = g.astype(F32) * o_ref[rows, cols].astype(F32)
            delta[half, :, into] = jnp.sum(product.T, axis=0, keepdims=True)
    dq_sum[0] = jnp.zeros_like(dq_sum[0])
    for source, to in ((kv_ref, dkv_ref), (other_kv_ref, other_dkv_ref)):
        to[:, HALF:, :] = jnp.zeros((8, HALF, 2 * HEAD_DIM), BF16)
        for k in range(0, 8, 2):
            keys = source[k : k + 2, :HALF, :HEAD_DIM].reshape(2 * HALF, HEAD_DIM)
            values = source[k : k + 2, :HALF, HEAD_DIM:].reshape(2 * HALF, HEAD_DIM)
            query_grad, key_grad, value_grad = tile(
                qs[1], gs[1], norm[1], delta[1], keys, values, None
            )
            if k or source is not kv_ref:
                dq_sum[1] += query_grad
            else:
                dq_sum[1] = query_grad
            key_grad = key_grad.astype(BF16).reshape(2, HALF, HEAD_DIM)
            value_grad = value_grad.astype(BF16).reshape(2, HALF, HEAD_DIM)
            to[k : k + 2, :HALF, :HEAD_DIM] = key_grad
            to[k : k + 2, :HALF, HEAD_DIM:] = value_grad


def rest_kernel(
    where_ref, qs, gs, norm, delta, dq_in, kv_ref, other_kv_ref, dkv_in, other_dkv_in,
    dq_ref, mine_ref, yours_ref, dq_sum, kv, dkv_ref,
):
    c, core = where_ref[0], where_ref[3]
    heads = dq_ref.shape[1] // HEAD_DIM
    scale = HEAD_DIM**-0.5
    kv[0], kv[1] = kv_ref[...], other_kv_ref[...]
    dkv_ref[0], dkv_ref[1] = dkv_in[...], other_dkv_in[...]
    dq_sum[...] = dq_in[...]
    side = (2 * HALF, heads * HALF)
    key_at = lax.broadcasted_iota(jnp.int32, side, 0)
    query_at = lax.broadcasted_iota(jnp.int32, side, 1) % HALF
    ahead = query_at - key_at % HALF
    second = key_at >= HALF

    def unit(i):
        late = (i > lax.div(c, 2)).astype(jnp.int32)
        k = i - late
        first = pl.multiple_of(late * HALF, HALF)
        behind = [
            jnp.where(s == c, 0, jnp.where((s < c) == (late == 0), -HALF, HALF))
            for s in (2 * k + core, 2 * k + 1 - core)
        ]
        visible = ahead >= jnp.where(second, behind[1], behind[0])
        keys = kv[:, k, pl.ds(first, HALF), :HEAD_DIM].reshape(2 * HALF, HEAD_DIM)
        values = kv[:, k, pl.ds(first, HALF), HEAD_DIM:].reshape(2 * HALF, HEAD_DIM)
        query_grad, key_grad, value_grad = tile(
            qs[late], gs[late], norm[late], delta[late], keys, values, visible
        )
        return late, k, first, query_grad, jnp.concatenate([key_grad, value_grad], 1)

    def stored(late, k, first, query_grad, now):
        dq_sum[late] += query_grad
        at = (slice(None), k, pl.ds(first, HALF), slice(None))
        before = dkv_ref[at].astype(F32).reshape(now.shape)
        dkv_ref[at] = (before + now).astype(BF16).reshape(2, HALF, now.shape[1])

    for first in range(0, 9, 3):
        for done in [unit(i) for i in range(first, first + 3)]:
            stored(*done)
    mine_ref[...] = dkv_ref[0]
    yours_ref[...] = dkv_ref[1]
    for half in range(2):
        for h in range(heads):
            dq_ref[half * HALF : (half + 1) * HALF, h * HEAD_DIM : (h + 1) * HEAD_DIM] = (
                dq_sum[half, h * HALF : (h + 1) * HALF, :] * scale
            ).astype(BF16)


def late_call(q, o, g, log_norm, kv, other_kv):
    side = q.shape[1] // HEAD_DIM * HALF
    vmem = pl.BlockSpec(memory_space=pltpu.VMEM)
    stacked = jax.ShapeDtypeStruct((2, side, HEAD_DIM), BF16)
    line = jax.ShapeDtypeStruct((2, 1, side), F32)
    half = jax.ShapeDtypeStruct(kv.shape, BF16)
    return pl.pallas_call(
        late_kernel,
        out_shape=(
            stacked,
            stacked,
            line,
            line,
            jax.ShapeDtypeStruct((2, side, HEAD_DIM), F32),
            half,
            half,
        ),
        in_specs=[vmem] * 6,
        out_specs=(vmem,) * 7,
        compiler_params=pltpu.CompilerParams(vmem_limit_bytes=24 * 1024 * 1024),
        cost_estimate=pl.CostEstimate(
            flops=10**10, bytes_accessed=2**22, transcendentals=10**6
        ),
    )(q, o, g, log_norm, kv, other_kv)


def rest_call(where, kept, kv, other_kv):
    qs, gs, norm, delta, dq, dkv, other_dkv = kept
    side = qs.shape[1]
    vmem = pl.BlockSpec(memory_space=pltpu.VMEM)
    half = jax.ShapeDtypeStruct(dkv.shape, BF16)
    return pl.pallas_call(
        rest_kernel,
        out_shape=(jax.ShapeDtypeStruct((2 * HALF, side), BF16), half, half),
        in_specs=[pl.BlockSpec(memory_space=pltpu.SMEM)] + [vmem] * 9,
        out_specs=(vmem,) * 3,
        scratch_shapes=[
            pltpu.VMEM((2, side, HEAD_DIM), F32),
            pltpu.VMEM((2, *kv.shape), BF16),
            pltpu.VMEM((2, *dkv.shape), BF16),
        ],
        compiler_params=pltpu.CompilerParams(vmem_limit_bytes=24 * 1024 * 1024),
        cost_estimate=pl.CostEstimate(
            flops=10**10, bytes_accessed=2**22, transcendentals=10**6
        ),
    )(where, qs, gs, norm, delta, dq, kv, other_kv, dkv, other_dkv)


def local(q, k, v, o, log_norm, dy, w, down, up):
    ylo, x, core, yhi, z = (lax.axis_index(a) for a in CTX + TP)
    where = jnp.stack([ylo * 8 + x * 2 + core, yhi, z, core]).astype(jnp.int32)
    together = lax.optimization_barrier
    own_blocks = gathered_round(dy, "z", True)
    mixed = lax.dot_general(down, o, (((0,), (1,)), ((), ())), preferred_element_type=F32)
    mixed = jnp.concatenate([mixed[i * 16 : i * 16 + 16] for i in range(4)], 1)
    peer = turned(dy, "yhi", 1)
    other = turned(mixed.astype(BF16), "yhi", 1)
    peer = jnp.concatenate([peer, (mixed + other.astype(F32)).astype(BF16)], 1)
    kv, own_blocks[1], own_blocks[7], peer = together(
        (jnp.concatenate([k, v], 1), own_blocks[1], own_blocks[7], peer)
    )
    kv = lax.all_to_all(jnp.broadcast_to(kv[None], (8,) + kv.shape), CTX[:2], 0, 0)
    own_blocks, kv = together((own_blocks, kv))
    other_kv = turned(kv, "core", 1)
    own_rows, own_cots = own_call(where, own_blocks, up)
    peer_blocks = gathered_round(peer, "z", False)
    peer_rows, cots, mine, yours = adapter_call(where, peer_blocks, up, own_rows, own_cots, o)
    low = (mine + turned(yours, "core", 1).astype(F32)).astype(BF16)
    cots, low = together((cots, low))
    g = gradient_call(where, own_rows, peer_rows, w, cots, down.T)
    other, g = together((turned(low, "ylo", 1), g))
    low = (low.astype(F32) + other.astype(F32)).astype(BF16)
    low, g = together((low, g))
    kept = late_call(q, o, g, log_norm, kv, other_kv)
    other = lax.ppermute(low, "x", [(i, i ^ 1) for i in range(4)])
    other, kept = together((other, kept))
    low = (low.astype(F32) + other.astype(F32)).astype(BF16)
    low, kept = together((low, kept))
    dq, mine, yours = rest_call(where, kept, kv, other_kv)
    other = lax.ppermute(low, "x", [(i, 3 - i) for i in range(4)])
    other, mine, yours = together((other, mine, yours))
    low = (low.astype(F32) + other.astype(F32)).astype(BF16)
    other = turned(low, "core", 1)
    mine = (mine.astype(F32) + turned(yours, "core", 1).astype(F32)).astype(BF16)
    other, mine = together((other, mine))
    pieces = lax.all_to_all(mine, CTX[:2], 0, 0)
    first, second = jnp.where(core == 0, low, other), jnp.where(core == 0, other, low)
    cut = low.shape[1] - 256
    down_grad = jnp.concatenate([first[:, cut:], second[:, cut:]], 1).astype(F32).T
    up_total = jnp.concatenate([first[:, :cut], second[:, :cut]], 1)
    before, after = turned(up_total, "z", 1), turned(up_total, "z", -1)
    far = (turned(before[:, :cut], "z", 1), turned(after[:, cut:], "z", -1))
    up_grad = placed_round(where, [up_total, after, *far, before])
    dkv_sum, low = summed(pieces)
    other = lax.ppermute(low, "z", [(i, i ^ 1) for i in range(8)])
    dkv_sum = (dkv_sum + other.astype(F32)).astype(BF16)
    return dq, dkv_sum[:, :128], dkv_sum[:, 128:], down_grad, up_grad


def solution(mesh):
    fine = Mesh(mesh.devices.reshape(SIZES), CTX + TP)
    placed = (
        P(CTX, TP),
        P(CTX, TP),
        P(CTX, TP),
        P(CTX, TP),
        P(TP, CTX),
        P(CTX + TP, None),
        P(TP, None),
        P(TP, None),
        P(),
    )
    return jax.shard_map(
        local,
        mesh=fine,
        in_specs=placed,
        out_specs=(P(CTX, TP), P(CTX, TP), P(CTX, TP), P(TP, None), P()),
        check_vma=False,
    )
```
